32 devices in a mesh: dp: 4 (over y, x), expert: 8 (over z, core).
Axes of the slice: x: 2, y: 2, z: 4, core: 2. Of those that a mesh axis runs over, the one named last changes fastest.
Arguments:
- tokens: bfloat16 [32768, 2048], P(('dp', 'expert')), may hold values from -16 to 16
- slot_param: bfloat16 [2048, 64], replicated, may hold values from -10 to 10
- pattern: int32 [64, 256], P(None, ('dp', 'expert')), may hold values from 0 to 1, as said below
- w_in: bfloat16 [16, 2048, 4096], P('expert', None, 'dp'), may hold values from -0.125 to 0.125
- w_out: bfloat16 [16, 4096, 2048], P('expert', 'dp'), may hold values from -0.09375 to 0.09375
Outputs:
- mixed: bfloat16 [32768, 2048], P(('dp', 'expert'))
The draws below stay inside these ranges and needn't reach their ends.
Inputs may be any that keep to these rules, and one draw needn't show every extreme that they name: `pattern`: every slot sees at least one block; about a quarter of all pairs are 1.
All inputs are finite; a program needn't handle non-finite values.
Results may differ from the reference program's by a relative error of at most 0.0095.
Values may be sent and summed in bfloat16 or wider, within the bound.
A program may use at most 64 MiB of HBM per device.

```python
import math
import jax
import jax.numpy as jnp
from jax import lax

D = 2048
H = 4096
SLOTS = 4
BLOCK = 128
EXPERTS = 16
TOKENS = 32768


def forced_blocks(key):
    return jax.random.randint(jax.random.fold_in(key, 7), (EXPERTS * SLOTS,), 0, TOKENS // BLOCK)


def draw_pattern(key, part):
    nblocks = TOKENS // BLOCK
    picks = jax.random.randint(jax.random.fold_in(key, 3), (EXPERTS * SLOTS, nblocks), 0, 4)
    base = (picks == 0).astype(jnp.int32)
    forced = forced_blocks(key)
    marked = (jnp.arange(nblocks)[None, :] == forced[:, None]).astype(jnp.int32)
    return jnp.maximum(base, marked)


def draw_tokens(key, part):
    return jnp.clip(jax.random.normal(jax.random.fold_in(key, 17), (TOKENS, D), jnp.float32), -6.0, 6.0).astype(jnp.bfloat16)


def draw_slot_param(key, part):
    width = EXPERTS * SLOTS
    scale = 3.0 / math.sqrt(D)
    return (jnp.clip(jax.random.normal(jax.random.fold_in(key, 23), (D, width), jnp.float32), -6.0, 6.0) * scale).astype(jnp.bfloat16)


def level_of(own_key, shape, cuts, low, top_value):
    def one(position, parts):
        steps = jax.random.uniform(jax.random.fold_in(jax.random.fold_in(own_key, 6), position), (parts,), jnp.float32, low / len(cuts), top_value / len(cuts))
        return jnp.repeat(jnp.exp(steps), shape[position] // parts).reshape((-1,) + (1,) * (len(shape) - position - 1))

    loudness = one(*cuts[0])
    for cut in cuts[1:]:
        loudness = loudness * one(*cut)
    return loudness


def scatter_about(stream_key, shape, scale, reach, pieces=(), kind=jnp.bfloat16):
    drawn = jax.random.normal(stream_key, shape, jnp.float32) * scale
    if len(pieces) > 0:
        drawn = level_of(stream_key, shape, pieces, -0.22, 0.18) * drawn
    return jnp.clip(drawn, min=-reach, max=reach).astype(kind)


def setup_inputs(seed: int = 0) -> dict:
    splits = jax.random.split(jax.random.key(seed), 6)
    return {
        "tokens": draw_tokens(jax.random.fold_in(splits[5], 71), 0),
        "slot_param": draw_slot_param(jax.random.fold_in(splits[5], 71), 0),
        "pattern": draw_pattern(jax.random.fold_in(splits[5], 71), 0),
        "w_in": scatter_about(splits[3], (EXPERTS, D, H), D ** -0.5, 0.125, ((0, 8), (2, 4))),
        "w_out": scatter_about(splits[4], (EXPERTS, H, D), H ** -0.5, 0.09375, ((0, 8), (1, 4))),
    }


floor_value = -1e30


def reference(tokens, slot_param, pattern, w_in, w_out):
    logits = jnp.dot(tokens, slot_param, preferred_element_type=jnp.float32)
    visible = jnp.repeat(pattern.T > 0, BLOCK, axis=0)
    slot_peak = jnp.max(jnp.where(visible, logits, floor_value), axis=0)
    weights = jnp.where(visible, jnp.exp(logits - slot_peak[None, :]), 0.0).astype(jnp.bfloat16)
    weight_sum = jnp.sum(weights.astype(jnp.float32), axis=0)
    numerator = lax.dot_general(weights, tokens, (((0,), (0,)), ((), ())), preferred_element_type=jnp.float32)
    slot_in = (numerator / weight_sum[:, None]).astype(jnp.bfloat16)
    grouped = slot_in.reshape(EXPERTS, SLOTS, D)

    def expert_mlp(inputs):
        rows, first, second = inputs
        hidden = jax.nn.gelu(jnp.dot(rows, first, preferred_element_type=jnp.float32)).astype(jnp.bfloat16)
        return jnp.dot(hidden, second, preferred_element_type=jnp.float32).astype(jnp.bfloat16)

    slot_out = lax.map(expert_mlp, (grouped, w_in, w_out)).reshape(EXPERTS * SLOTS, D)
    mixing = jax.nn.softmax(logits, axis=1).astype(jnp.bfloat16)
    block_rows = 4096 if TOKENS % 4096 == 0 else TOKENS
    blocked = mixing.reshape(TOKENS // block_rows, block_rows, EXPERTS * SLOTS)

    def combine(piece):
        return jnp.dot(piece, slot_out, preferred_element_type=jnp.float32).astype(jnp.bfloat16)

    return lax.map(combine, blocked).reshape(TOKENS, D)
```

```python
import functools

import jax
import jax.numpy as jnp
from jax import lax
from jax.experimental import pallas as pl
from jax.experimental.pallas import tpu as pltpu
from jax.sharding import PartitionSpec as P

MESH = pl.DeviceIdType.MESH
floor_value = -1e30
F32, BF16 = jnp.float32, jnp.bfloat16


def nt_dot(a, b):
    return lax.dot_general(a, b, (((1,), (1,)), ((), ())), preferred_element_type=F32)


def gelu(x):
    return 0.5 * x * (1.0 + jnp.tanh(0.7978845608028654 * (x + 0.044715 * (x * x * x))))


def fold(x):
    half = x.shape[1] // 2
    return jnp.concatenate([x[:, :half], x[:, half:]], axis=0).astype(BF16)


def unfold(x):
    rows = x.shape[0] // 2
    wide = x.astype(F32)
    return jnp.concatenate([wide[:rows], wide[rows:]], axis=1)


def slots_kernel(
    n_dp, n_ex, pieces,
    tok_hbm, slot_ref, pat_ref, win_hbm, wout_hbm,
    mix_ref, out_ref,
    tok, win, wout, logits, wts,
    stat1, num1, rstat1, rnum1,
    send2, recv2, xs, rx, part, rpart, own5, recv5, full6, recv6,
    tok_sem, w_sem,
    ss1, rs1, sn1, rn1, s2, r2, s3, r3, s4, r4, s5, r5, s6, r6,
):
    d, k = lax.axis_index("dp"), lax.axis_index("expert")
    slots, width = slot_ref.shape
    rows = tok.shape[0]
    cols = width // n_dp
    per_dev = slots // n_ex
    exp_dev, _, hid = win.shape
    blocks = pat_ref.shape[0]
    block = rows // blocks
    lanes = stat1.shape[1]
    piece = rows // pieces
    folded = recv5.dtype == BF16

    def to_dp(src, dst, ssem, rsem, i):
        return pltpu.make_async_remote_copy(
            src_ref=src, dst_ref=dst, send_sem=ssem.at[i], recv_sem=rsem.at[i],
            device_id={"dp": lax.rem(d + i, n_dp)}, device_id_type=MESH,
        )

    def to_ex(src, dst, ssem, rsem, i):
        return pltpu.make_async_remote_copy(
            src_ref=src, dst_ref=dst, send_sem=ssem.at[i], recv_sem=rsem.at[i],
            device_id={"expert": lax.rem(k + i, n_ex)}, device_id_type=MESH,
        )

    loads = [
        pltpu.make_async_copy(
            tok_hbm.at[pl.ds(c * piece, piece)], tok.at[pl.ds(c * piece, piece)], tok_sem.at[c]
        )
        for c in range(pieces)
    ]
    for load in loads:
        load.start()
    barrier = pltpu.get_barrier_semaphore()
    for i in range(1, n_dp):
        pl.semaphore_signal(
            barrier, inc=1, device_id={"dp": lax.rem(d + i, n_dp)}, device_id_type=MESH
        )
    for i in range(1, n_ex):
        pl.semaphore_signal(
            barrier, inc=1, device_id={"expert": lax.rem(k + i, n_ex)}, device_id_type=MESH
        )
    load_in = pltpu.make_async_copy(win_hbm, win, w_sem.at[0])
    load_out = pltpu.make_async_copy(wout_hbm, wout, w_sem.at[1])

    row_id = lax.broadcasted_iota(jnp.int32, (slots, lanes), 0)
    lane_id = lax.broadcasted_iota(jnp.int32, (slots, lanes), 1)
    eye = row_id == lane_id

    def as_column(row):
        return jnp.sum(jnp.where(eye, row, 0.0), axis=1, keepdims=True)

    def as_row(column):
        return jnp.sum(jnp.where(eye, column, 0.0), axis=0, keepdims=True)

    slot_t = slot_ref[...]
    for c in range(pieces):
        loads[c].wait()
        if c == pieces - 1:
            load_in.start()
            load_out.start()
        logits[:, c * piece:(c + 1) * piece] = nt_dot(slot_t, tok[c * piece:(c + 1) * piece, :])

    seen = pat_ref[...].astype(F32)
    if lanes > slots:
        seen = jnp.concatenate([seen, jnp.zeros((blocks, lanes - slots), F32)], axis=1)
    columns = [as_column(seen[b:b + 1, :]) > 0.0 for b in range(blocks)]
    masked = [
        jnp.where(columns[b], logits[:, b * block:(b + 1) * block], floor_value)
        for b in range(blocks)
    ]
    top = masked[0]
    for b in range(1, blocks):
        top = jnp.maximum(top, masked[b])
    peak = jnp.max(top, axis=1, keepdims=True)
    total = jnp.zeros((slots, block), F32)
    for b in range(blocks):
        shifted = jnp.where(columns[b], masked[b] - peak, floor_value)
        weight = jnp.exp(shifted).astype(BF16)
        wts[:, b * block:(b + 1) * block] = weight
        total = total + weight.astype(F32)
    den = jnp.sum(total, axis=1, keepdims=True)
    stat_row = lax.broadcasted_iota(jnp.int32, stat1.shape, 0)
    stat1[...] = jnp.where(stat_row == 0, as_row(peak), as_row(den))

    pl.semaphore_wait(barrier, n_dp - 1 + n_ex - 1)
    stat_copies = [to_dp(stat1, rstat1.at[i], ss1, rs1, i) for i in range(1, n_dp)]
    for copy in stat_copies:
        copy.start()
    weights = wts[...]
    num_copies = []
    for i in list(range(1, n_dp)) + [0]:
        target = lax.rem(d + i, n_dp)
        strip = tok[:, pl.ds(pl.multiple_of(target * cols, cols), cols)]
        num1[i] = jnp.dot(weights, strip, preferred_element_type=F32).astype(BF16)
        if i:
            copy = to_dp(num1.at[i], rnum1.at[i], sn1, rn1, i)
            copy.start()
            num_copies.append(copy)

    raw = logits[...]
    risen = jnp.exp(raw - jnp.max(raw, axis=0, keepdims=True))
    mix_ref[...] = (risen / jnp.sum(risen, axis=0, keepdims=True)).astype(BF16)

    for copy in stat_copies:
        copy.wait_recv()
    stats = [stat1[...]] + [rstat1[i] for i in range(1, n_dp)]
    group_peak = stats[0][0:1]
    for stat in stats[1:]:
        group_peak = jnp.maximum(group_peak, stat[0:1])
    scales = [jnp.exp(stat[0:1] - group_peak) for stat in stats]
    group_den = stats[0][1:2] * scales[0]
    for stat, scale in zip(stats[1:], scales[1:]):
        group_den = group_den + stat[1:2] * scale
    scales = [as_column(scale) for scale in scales]
    tail = jnp.where(lane_id == 0, as_column(group_peak), as_column(group_den))
    send2[:, :, cols:] = tail.reshape(n_ex, per_dev, lanes)
    group_num = scales[0] * num1[0].astype(F32)
    for i in range(1, n_dp):
        num_copies[i - 1].wait_recv()
        group_num = group_num + scales[i] * rnum1[i].astype(F32)
    send2[:, :, :cols] = group_num.reshape(n_ex, per_dev, cols)

    copies2 = []
    for i in range(1, n_ex):
        copy = to_ex(send2.at[lax.rem(k + i, n_ex)], recv2.at[i], s2, r2, i)
        copy.start()
        copies2.append(copy)
    for copy in copies2:
        copy.wait_recv()
    given = [send2[k]] + [recv2[i] for i in range(1, n_ex)]
    last_peak = given[0][:, cols:cols + 1]
    for item in given[1:]:
        last_peak = jnp.maximum(last_peak, item[:, cols:cols + 1])
    num = jnp.zeros((per_dev, cols), F32)
    den = jnp.zeros((per_dev, 1), F32)
    for item in given:
        scale = jnp.exp(item[:, cols:cols + 1] - last_peak)
        num = num + scale * item[:, :cols]
        den = den + scale * item[:, cols + 1:cols + 2]
    xs[...] = (num / den).astype(BF16).astype(F32)

    copies3 = [to_dp(xs, rx.at[i], s3, r3, i) for i in range(1, n_dp)]
    for copy in copies3:
        copy.start()
    load_in.wait()
    sums = [jnp.zeros((per_dev, hid), F32) for _ in range(exp_dev)]
    for i in range(n_dp):
        if i:
            copies3[i - 1].wait_recv()
        x = (rx[i] if i else xs[...]).astype(BF16)
        start = pl.multiple_of(lax.rem(d + n_dp - i, n_dp) * cols, cols)
        for e in range(exp_dev):
            sums[e] = sums[e] + jnp.dot(
                x, win[e, pl.ds(start, cols), :], preferred_element_type=F32
            )
    hidden = [gelu(s).astype(BF16) for s in sums]
    load_out.wait()
    own_slots = per_dev // exp_dev
    owner = lax.broadcasted_iota(jnp.int32, (per_dev, cols), 0) // own_slots
    copies4 = []
    for i in list(range(1, n_dp)) + [0]:
        start = pl.multiple_of(lax.rem(d + i, n_dp) * cols, cols)
        value = jnp.zeros((per_dev, cols), F32)
        for e in range(exp_dev):
            made = jnp.dot(hidden[e], wout[e, :, pl.ds(start, cols)], preferred_element_type=F32)
            value = jnp.where(owner == e, made, value)
        part[i] = value
        if i:
            copy = to_dp(part.at[i], rpart.at[i], s4, r4, i)
            copy.start()
            copies4.append(copy)
    value = part[0]
    for i in range(1, n_dp):
        copies4[i - 1].wait_recv()
        value = value + rpart[i]

    own5[...] = fold(value) if folded else value.astype(BF16).astype(F32)
    copies5 = [to_ex(own5, recv5.at[i], s5, r5, i) for i in range(1, n_ex)]
    for copy in copies5:
        copy.start()
    for copy in copies2:
        copy.wait_send()
    for i in range(n_ex):
        if i:
            copies5[i - 1].wait_recv()
        item = recv5[i] if i else own5[...]
        source = lax.rem(k + n_ex - i, n_ex)
        send2[source, :, :cols] = unfold(item) if folded else item
    full6[...] = send2[:, :, :cols].reshape(slots, cols).astype(BF16)
    copies6 = [to_dp(full6, recv6.at[i], s6, r6, i) for i in range(1, n_dp)]
    for copy in copies6:
        copy.start()
    for i in range(n_dp):
        if i:
            copies6[i - 1].wait_recv()
        start = pl.multiple_of(lax.rem(d + n_dp - i, n_dp) * cols, cols)
        out_ref[:, pl.ds(start, cols)] = recv6[i] if i else full6[...]
    for copy in stat_copies + num_copies + copies3 + copies4 + copies5 + copies6:
        copy.wait_send()


def local(n_dp, n_ex, tokens, slot_param, pattern, w_in, w_out):
    rows, width = tokens.shape
    slots = slot_param.shape[1]
    cols = width // n_dp
    per_dev = slots // n_ex
    lanes = -(-slots // 128) * 128
    pieces = 4
    item = ((2 * per_dev, cols // 2), BF16) if cols % 256 == 0 else ((per_dev, cols), F32)
    dma = pltpu.SemaphoreType.DMA
    vmem, anywhere = pl.BlockSpec(memory_space=pltpu.VMEM), pl.BlockSpec(memory_space=pl.ANY)
    mixing, slot_out = pl.pallas_call(
        functools.partial(slots_kernel, n_dp, n_ex, pieces),
        out_shape=(
            jax.ShapeDtypeStruct((slots, rows), BF16),
            jax.ShapeDtypeStruct((slots, width), BF16),
        ),
        in_specs=[anywhere, vmem, vmem, anywhere, anywhere],
        out_specs=(vmem, vmem),
        scratch_shapes=[
            pltpu.VMEM((rows, width), BF16),
            pltpu.VMEM(w_in.shape, BF16),
            pltpu.VMEM(w_out.shape, BF16),
            pltpu.VMEM((slots, rows), F32),
            pltpu.VMEM((slots, rows), BF16),
            pltpu.VMEM((8, lanes), F32),
            pltpu.VMEM((n_dp, slots, cols), BF16),
            pltpu.VMEM((n_dp, 8, lanes), F32),
            pltpu.VMEM((n_dp, slots, cols), BF16),
            pltpu.VMEM((n_ex, per_dev, cols + lanes), F32),
            pltpu.VMEM((n_ex, per_dev, cols + lanes), F32),
            pltpu.VMEM((per_dev, cols), F32),
            pltpu.VMEM((n_dp, per_dev, cols), F32),
            pltpu.VMEM((n_dp, per_dev, cols), F32),
            pltpu.VMEM((n_dp, per_dev, cols), F32),
            pltpu.VMEM(*item),
            pltpu.VMEM((n_ex,) + item[0], item[1]),
            pltpu.VMEM((slots, cols), BF16),
            pltpu.VMEM((n_dp, slots, cols), BF16),
            dma((pieces,)),
            dma((2,)),
        ]
        + [dma((n,)) for n in (n_dp, n_dp, n_ex, n_dp, n_dp, n_ex, n_dp) for _ in range(2)],
        compiler_params=pltpu.CompilerParams(
            collective_id=0, has_side_effects=True, vmem_limit_bytes=60 * 1024 * 1024
        ),
        cost_estimate=pl.CostEstimate(
            flops=4 * rows * width * slots + 4 * per_dev * w_in.size // w_in.shape[0],
            bytes_accessed=2 * (tokens.size + w_in.size + w_out.size),
            transcendentals=2 * rows * slots,
        ),
    )(tokens, slot_param.T, pattern.T, w_in, w_out)
    result = lax.dot_general(
        mixing, slot_out, (((0,), (0,)), ((), ())), preferred_element_type=F32
    )
    return result.astype(BF16)


def solution(mesh):
    return jax.shard_map(
        functools.partial(local, mesh.shape["dp"], mesh.shape["expert"]),
        mesh=mesh,
        in_specs=(
            P(("dp", "expert"), None),
            P(),
            P(None, ("dp", "expert")),
            P("expert", None, "dp"),
            P("expert", "dp", None),
        ),
        out_specs=P(("dp", "expert"), None),
        check_vma=False,
    )
```

```python
import functools

import jax
import jax.numpy as jnp
from jax import lax
from jax.experimental import pallas as pl
from jax.experimental.pallas import tpu as pltpu
from jax.sharding import PartitionSpec as P

MESH = pl.DeviceIdType.MESH
floor_value = -1e30
F32, BF16 = jnp.float32, jnp.bfloat16


def nt_dot(a, b):
    return lax.dot_general(a, b, (((1,), (1,)), ((), ())), preferred_element_type=F32)


def gelu(x):
    return 0.5 * x * (1.0 + jnp.tanh(0.7978845608028654 * (x + 0.044715 * (x * x * x))))


def fold(x):
    half = x.shape[1] // 2
    return jnp.concatenate([x[:, :half], x[:, half:]], axis=0).astype(BF16)


def flip(me, i, n):
    if n & (n - 1):
        return lax.rem(me + i, n), lax.rem(me + n - i, n)
    other, bit = 0, 1
    while bit < n:
        own = lax.rem(me // bit, 2)
        other = other + bit * ((1 - own) if i & bit else own)
        bit *= 2
    return other, other


def unfold(x):
    rows = x.shape[0] // 2
    wide = x.astype(F32)
    return jnp.concatenate([wide[:rows], wide[rows:]], axis=1)


def slots_kernel(
    n_dp, n_ex, pieces,
    tok_hbm, slot_hbm, pat_hbm, win_hbm, wout_hbm,
    out_ref,
    slot_ref, pat_ref, tok, win, wout, logits, wts, mix,
    stat1, rstat1, num1, rnum1, stat2, rstat2,
    send2, recv2, xs, rx, part, rpart, own5, recv5, recv6,
    tok_sem, w_sem,
    ss1, rs1, sn1, rn1, ss2, rs2, s2, r2, s3, r3, s4, r4, s5, r5, s6, r6,
):
    d, k = lax.axis_index("dp"), lax.axis_index("expert")
    slots, width = slot_ref.shape
    rows = tok.shape[0]
    cols = width // n_dp
    per_dev = slots // n_ex
    exp_dev, _, hid = win.shape
    blocks = pat_ref.shape[0]
    block = rows // blocks
    lanes = stat1.shape[1]
    piece = rows // pieces
    folded = recv5.dtype == BF16

    dp_to, dp_from = zip(*[flip(d, i, n_dp) for i in range(n_dp)])
    ex_to, ex_from = zip(*[flip(k, i, n_ex) for i in range(n_ex)])

    def to_dp(src, dst, ssem, rsem, i):
        return pltpu.make_async_remote_copy(
            src_ref=src, dst_ref=dst, send_sem=ssem, recv_sem=rsem,
            device_id={"dp": dp_to[i]}, device_id_type=MESH,
        )

    def to_ex(src, dst, ssem, rsem, i):
        return pltpu.make_async_remote_copy(
            src_ref=src, dst_ref=dst, send_sem=ssem, recv_sem=rsem,
            device_id={"expert": ex_to[i]}, device_id_type=MESH,
        )

    def strip(index):
        return pl.ds(pl.multiple_of(index * cols, cols), cols)

    def launch(copies):
        for copy in copies:
            copy.start()
        return copies

    loads = [
        pltpu.make_async_copy(
            tok_hbm.at[pl.ds(c * piece, piece)], tok.at[pl.ds(c * piece, piece)], tok_sem.at[c]
        )
        for c in range(pieces)
    ]
    load_slot = pltpu.make_async_copy(slot_hbm, slot_ref, w_sem.at[2])
    load_pat = pltpu.make_async_copy(pat_hbm, pat_ref, w_sem.at[3])
    for load in [load_slot, load_pat] + loads:
        load.start()
    barrier = pltpu.get_barrier_semaphore()
    for i in range(1, n_dp):
        pl.semaphore_signal(
            barrier, inc=1, device_id={"dp": dp_to[i]}, device_id_type=MESH
        )
    for i in range(1, n_ex):
        pl.semaphore_signal(
            barrier, inc=1, device_id={"expert": ex_to[i]}, device_id_type=MESH
        )
    load_in = pltpu.make_async_copy(win_hbm, win, w_sem.at[0])
    load_out = pltpu.make_async_copy(wout_hbm, wout, w_sem.at[1])

    row_id = lax.broadcasted_iota(jnp.int32, (slots, lanes), 0)
    lane_id = lax.broadcasted_iota(jnp.int32, (slots, lanes), 1)
    eye = row_id == lane_id

    def as_column(row):
        return jnp.sum(jnp.where(eye, row, 0.0), axis=1, keepdims=True)

    def as_row(column):
        return jnp.sum(jnp.where(eye, column, 0.0), axis=0, keepdims=True)

    load_slot.wait()
    load_pat.wait()
    slot_t = slot_ref[...]
    for c in range(pieces):
        loads[c].wait()
        if c == pieces - 1:
            load_in.start()
            load_out.start()
        logits[:, c * piece:(c + 1) * piece] = nt_dot(slot_t, tok[c * piece:(c + 1) * piece, :])

    seen = pat_ref[...].astype(F32)
    if lanes > slots:
        seen = jnp.concatenate([seen, jnp.zeros((blocks, lanes - slots), F32)], axis=1)
    columns = [as_column(seen[b:b + 1, :]) > 0.0 for b in range(blocks)]
    masked = [
        jnp.where(columns[b], logits[:, b * block:(b + 1) * block], floor_value)
        for b in range(blocks)
    ]
    top = masked[0]
    for b in range(1, blocks):
        top = jnp.maximum(top, masked[b])
    peak = jnp.max(top, axis=1, keepdims=True)
    total = jnp.zeros((slots, block), F32)
    for b in range(blocks):
        shifted = jnp.where(columns[b], masked[b] - peak, floor_value)
        weight = jnp.exp(shifted).astype(BF16)
        wts[:, b * block:(b + 1) * block] = weight
        total = total + weight.astype(F32)
    den = jnp.sum(total, axis=1, keepdims=True)
    stat_row = lax.broadcasted_iota(jnp.int32, stat1.shape, 0)
    stat1[...] = jnp.where(stat_row == 0, as_row(peak), as_row(den))

    pl.semaphore_wait(barrier, n_dp - 1 + n_ex - 1)
    dp_far = list(range(n_dp - 1, 0, -1))
    ex_far = list(range(n_ex - 1, 0, -1))
    stat_copies = launch(
        [to_dp(stat1, rstat1.at[i], ss1.at[i], rs1.at[i], i) for i in dp_far]
    )
    weights = wts[...]
    num_copies = {}
    for i in dp_far + [0]:
        num1[i] = jnp.dot(
            weights, tok[:, strip(dp_to[i])], preferred_element_type=F32
        ).astype(BF16)
        if i:
            num_copies[i] = to_dp(num1.at[i], rnum1.at[i], sn1.at[i], rn1.at[i], i)
            num_copies[i].start()

    for copy in stat_copies:
        copy.wait_recv()

    def join(stats):
        high = stats[0][0:1]
        for stat in stats[1:]:
            high = jnp.maximum(high, stat[0:1])
        low = stats[0][1:2] * jnp.exp(stats[0][0:1] - high)
        for stat in stats[1:]:
            low = low + stat[1:2] * jnp.exp(stat[0:1] - high)
        return high, low

    stats = [stat1[...]] + [rstat1[i] for i in range(1, n_dp)]
    high, low = join(stats)
    stat2[...] = jnp.where(stat_row == 0, high, low)
    stat2_copies = launch(
        [to_ex(stat2, rstat2.at[i], ss2.at[i], rs2.at[i], i) for i in ex_far]
    )

    raw = logits[...]
    risen = jnp.exp(raw - jnp.max(raw, axis=0, keepdims=True))
    mix[...] = (risen / jnp.sum(risen, axis=0, keepdims=True)).T.astype(BF16)

    for copy in stat2_copies:
        copy.wait_recv()
    high, low = join([stat2[...]] + [rstat2[i] for i in range(1, n_ex)])
    scales = [as_column(jnp.exp(stat[0:1] - high) / low) for stat in stats]
    joint = scales[0] * num1[0].astype(F32)
    for i in range(1, n_dp):
        num_copies[i].wait_recv()
        joint = joint + scales[i] * rnum1[i].astype(F32)
    joint = joint.reshape(n_ex, per_dev, cols)
    if folded:
        joint = jnp.concatenate([joint[:, :, :cols // 2], joint[:, :, cols // 2:]], axis=1)
    send2[...] = joint.astype(send2.dtype)

    copies2 = launch(
        [to_ex(send2.at[ex_to[i]], recv2.at[i], s2.at[i], r2.at[i], i) for i in ex_far]
    )
    value = send2[k].astype(F32)
    for copy in copies2:
        copy.wait_recv()
    for i in range(1, n_ex):
        value = value + recv2[i].astype(F32)
    xs[...] = value.astype(BF16).astype(xs.dtype)

    copies3 = launch([to_dp(xs, rx.at[i], s3.at[i], r3.at[i], i) for i in range(1, n_dp)])
    load_in.wait()
    sums = [jnp.zeros((per_dev, hid), F32) for _ in range(exp_dev)]
    for i in range(n_dp):
        if i:
            copies3[i - 1].wait_recv()
        x = rx[i] if i else xs[...]
        x = (unfold(x) if folded else x).astype(BF16)
        start = pl.multiple_of(dp_from[i] * cols, cols)
        for e in range(exp_dev):
            sums[e] = sums[e] + jnp.dot(
                x, win[e, pl.ds(start, cols), :], preferred_element_type=F32
            )
    hidden = [gelu(s).astype(BF16) for s in sums]
    load_out.wait()
    own_slots = per_dev // exp_dev
    owner = lax.broadcasted_iota(jnp.int32, (per_dev, cols), 0) // own_slots
    copies4 = {}
    for i in dp_far + [0]:
        value = jnp.zeros((per_dev, cols), F32)
        for e in range(exp_dev):
            made = jnp.dot(hidden[e], wout[e, :, strip(dp_to[i])], preferred_element_type=F32)
            value = jnp.where(owner == e, made, value)
        part[i] = value
        if i:
            copies4[i] = to_dp(part.at[i], rpart.at[i], s4.at[i], r4.at[i], i)
            copies4[i].start()
    value = part[0]
    for i in range(1, n_dp):
        copies4[i].wait_recv()
        value = value + rpart[i]

    own5[...] = fold(value) if folded else value.astype(BF16).astype(F32)
    copies5 = launch(
        [to_ex(own5, recv5.at[i], s5.at[i], r5.at[i], i) for i in range(1, n_ex)]
    )
    copies6 = {}
    for b in range(n_ex):
        if b:
            copies5[b - 1].wait_recv()
        block_ref = recv5.at[b] if b else own5
        for i in dp_far:
            copies6[i, b] = to_dp(block_ref, recv6.at[i, b], s6.at[i, b], r6.at[i, b], i)
            copies6[i, b].start()
    for copy in copies2:
        copy.wait_send()
    mixing = mix[...]
    for i in range(n_dp):
        for b in range(n_ex):
            if i:
                copies6[i, b].wait_recv()
            item = recv6[i, b] if i else (recv5[b] if b else own5[...])
            send2[ex_from[b]] = item
        table = send2[...].astype(F32)
        if folded:
            table = jnp.concatenate([table[:, :per_dev, :], table[:, per_dev:, :]], axis=2)
        table = table.reshape(slots, cols).astype(BF16)
        out_ref[:, strip(dp_from[i])] = jnp.dot(
            mixing, table, preferred_element_type=F32
        ).astype(BF16)
    for copy in (
        stat_copies + list(num_copies.values()) + stat2_copies + copies3
        + list(copies4.values()) + copies5 + list(copies6.values())
    ):
        copy.wait_send()


def local(n_dp, n_ex, tokens, slot_param, pattern, w_in, w_out):
    rows, width = tokens.shape
    slots = slot_param.shape[1]
    cols = width // n_dp
    per_dev = slots // n_ex
    lanes = -(-slots // 128) * 128
    pieces = 4
    item = ((2 * per_dev, cols // 2), BF16) if cols % 256 == 0 else ((per_dev, cols), F32)
    dma = pltpu.SemaphoreType.DMA
    vmem, in_hbm = pl.BlockSpec(memory_space=pltpu.VMEM), pl.BlockSpec(memory_space=pltpu.HBM)
    return pl.pallas_call(
        functools.partial(slots_kernel, n_dp, n_ex, pieces),
        out_shape=jax.ShapeDtypeStruct((rows, width), BF16),
        in_specs=[in_hbm] * 5,
        out_specs=vmem,
        scratch_shapes=[
            pltpu.VMEM((slots, width), BF16),
            pltpu.VMEM(pattern.shape[::-1], pattern.dtype),
            pltpu.VMEM((rows, width), BF16),
            pltpu.VMEM(w_in.shape, BF16),
            pltpu.VMEM(w_out.shape, BF16),
            pltpu.VMEM((slots, rows), F32),
            pltpu.VMEM((slots, rows), BF16),
            pltpu.VMEM((rows, slots), BF16),
            pltpu.VMEM((8, lanes), F32),
            pltpu.VMEM((n_dp, 8, lanes), F32),
            pltpu.VMEM((n_dp, slots, cols), BF16),
            pltpu.VMEM((n_dp, slots, cols), BF16),
            pltpu.VMEM((8, lanes), F32),
            pltpu.VMEM((n_ex, 8, lanes), F32),
            pltpu.VMEM((n_ex,) + item[0], item[1]),
            pltpu.VMEM((n_ex,) + item[0], item[1]),
            pltpu.VMEM(*item),
            pltpu.VMEM((n_dp,) + item[0], item[1]),
            pltpu.VMEM((n_dp, per_dev, cols), F32),
            pltpu.VMEM((n_dp, per_dev, cols), F32),
            pltpu.VMEM(*item),
            pltpu.VMEM((n_ex,) + item[0], item[1]),
            pltpu.VMEM((n_dp, n_ex) + item[0], item[1]),
            dma((pieces,)),
            dma((4,)),
        ]
        + [
            dma(shape)
            for shape in (
                (n_dp,), (n_dp,), (n_ex,), (n_ex,), (n_dp,), (n_dp,), (n_ex,), (n_dp, n_ex)
            )
            for _ in range(2)
        ],
        compiler_params=pltpu.CompilerParams(
            collective_id=0, has_side_effects=True, vmem_limit_bytes=48 * 1024 * 1024
        ),
        cost_estimate=pl.CostEstimate(
            flops=6 * rows * width * slots + 4 * per_dev * w_in.size // w_in.shape[0],
            bytes_accessed=2 * (tokens.size + w_in.size + w_out.size),
            transcendentals=2 * rows * slots,
        ),
    )(tokens, slot_param.T, pattern.T, w_in, w_out)


def solution(mesh):
    return jax.shard_map(
        functools.partial(local, mesh.shape["dp"], mesh.shape["expert"]),
        mesh=mesh,
        in_specs=(
            P(("dp", "expert"), None),
            P(),
            P(None, ("dp", "expert")),
            P("expert", None, "dp"),
            P("expert", "dp", None),
        ),
        out_specs=P(("dp", "expert"), None),
        check_vma=False,
    )
```

```python
import functools

import jax
import jax.numpy as jnp
from jax import lax
from jax.experimental import pallas as pl
from jax.experimental.pallas import tpu as pltpu
from jax.sharding import PartitionSpec as P

MESH = pl.DeviceIdType.MESH
floor_value = -1e30
F32, BF16 = jnp.float32, jnp.bfloat16


def nt_dot(a, b):
    return lax.dot_general(a, b, (((1,), (1,)), ((), ())), preferred_element_type=F32)


def gelu(x):
    return 0.5 * x * (1.0 + jnp.tanh(0.7978845608028654 * (x + 0.044715 * (x * x * x))))


def fold(x):
    half = x.shape[1] // 2
    return jnp.concatenate([x[:, :half], x[:, half:]], axis=0).astype(BF16)


def flip(me, i, n):
    if n & (n - 1):
        return lax.rem(me + i, n), lax.rem(me + n - i, n)
    other, bit = 0, 1
    while bit < n:
        own = lax.rem(me // bit, 2)
        other = other + bit * ((1 - own) if i & bit else own)
        bit *= 2
    return other, other


def unfold(x):
    rows = x.shape[0] // 2
    wide = x.astype(F32)
    return jnp.concatenate([wide[:rows], wide[rows:]], axis=1)


def slots_kernel(
    n_dp, n_ex, pieces,
    tok_hbm, slot_hbm, pat_hbm, win_hbm, wout_hbm,
    out_ref,
    slot_ref, pat_ref, tok, win, wout, logits, wts, mix,
    stat1, rstat1, num1, rnum1, stat2, rstat2,
    send2, recv2, xs, rx, part, rpart, own5, recv5, recv6,
    tok_sem, w_sem, a_sem,
    ss1, rs1, sn1, rn1, ss2, rs2, s2, r2, s3, r3, s4, r4, s5, r5, s6, r6,
):
    d, k = lax.axis_index("dp"), lax.axis_index("expert")
    slots, width = slot_ref.shape
    rows = tok.shape[0]
    cols = width // n_dp
    per_dev = slots // n_ex
    exp_dev, _, hid = win.shape
    blocks = pat_ref.shape[0]
    block = rows // blocks
    lanes = stat1.shape[1]
    piece = rows // pieces
    folded = recv5.dtype == BF16

    dp_to, dp_from = zip(*[flip(d, i, n_dp) for i in range(n_dp)])
    ex_to, ex_from = zip(*[flip(k, i, n_ex) for i in range(n_ex)])

    def to_dp(src, dst, ssem, rsem, i):
        return pltpu.make_async_remote_copy(
            src_ref=src, dst_ref=dst, send_sem=ssem, recv_sem=rsem,
            device_id={"dp": dp_to[i]}, device_id_type=MESH,
        )

    def to_ex(src, dst, ssem, rsem, i):
        return pltpu.make_async_remote_copy(
            src_ref=src, dst_ref=dst, send_sem=ssem, recv_sem=rsem,
            device_id={"expert": ex_to[i]}, device_id_type=MESH,
        )

    def strip(index):
        return pl.ds(pl.multiple_of(index * cols, cols), cols)

    def launch(copies):
        for copy in copies:
            copy.start()
        return copies

    loads = [
        pltpu.make_async_copy(
            tok_hbm.at[pl.ds(c * piece, piece)], tok.at[pl.ds(c * piece, piece)], tok_sem.at[c]
        )
        for c in range(pieces)
    ]
    load_slot = pltpu.make_async_copy(slot_hbm, slot_ref, a_sem.at[0])
    load_pat = pltpu.make_async_copy(pat_hbm, pat_ref, a_sem.at[1])
    for load in [load_slot, load_pat] + loads:
        load.start()
    barrier = pltpu.get_barrier_semaphore()
    for i in range(1, n_dp):
        pl.semaphore_signal(
            barrier, inc=1, device_id={"dp": dp_to[i]}, device_id_type=MESH
        )
    for i in range(1, n_ex):
        pl.semaphore_signal(
            barrier, inc=1, device_id={"expert": ex_to[i]}, device_id_type=MESH
        )

    def in_parts(src, dst, first):
        depth = src.shape[1] // 2
        return [
            pltpu.make_async_copy(
                src.at[e, pl.ds(h * depth, depth)], dst.at[e, pl.ds(h * depth, depth)],
                w_sem.at[first + 2 * e + h],
            )
            for e in range(exp_dev) for h in range(2)
        ]

    load_in = in_parts(win_hbm, win, 0)
    load_out = in_parts(wout_hbm, wout, 2 * exp_dev)

    row_id = lax.broadcasted_iota(jnp.int32, (slots, lanes), 0)
    lane_id = lax.broadcasted_iota(jnp.int32, (slots, lanes), 1)
    eye = row_id == lane_id

    def as_column(row):
        return jnp.sum(jnp.where(eye, row, 0.0), axis=1, keepdims=True)

    def as_row(column):
        return jnp.sum(jnp.where(eye, column, 0.0), axis=0, keepdims=True)

    load_slot.wait()
    load_pat.wait()
    slot_t = slot_ref[...]
    for c in range(pieces):
        loads[c].wait()
        if c == pieces - 1:
            launch(load_in + load_out)
        span = slice(c * piece, (c + 1) * piece)
        logits[:, span] = nt_dot(tok[span, :], slot_t).T

    seen = pat_ref[...].astype(F32)
    if lanes > slots:
        seen = jnp.concatenate([seen, jnp.zeros((blocks, lanes - slots), F32)], axis=1)
    columns = [as_column(seen[b:b + 1, :]) > 0.0 for b in range(blocks)]
    masked = [
        jnp.where(columns[b], logits[:, b * block:(b + 1) * block], floor_value)
        for b in range(blocks)
    ]
    top = masked[0]
    for b in range(1, blocks):
        top = jnp.maximum(top, masked[b])
    peak = jnp.max(top, axis=1, keepdims=True)
    total = jnp.zeros((slots, block), F32)
    for b in range(blocks):
        shifted = jnp.where(columns[b], masked[b] - peak, floor_value)
        weight = jnp.exp(shifted).astype(BF16)
        wts[:, b * block:(b + 1) * block] = weight
        total = total + weight.astype(F32)
    den = jnp.sum(total, axis=1, keepdims=True)
    stat_row = lax.broadcasted_iota(jnp.int32, stat1.shape, 0)
    stat1[...] = jnp.where(stat_row == 0, as_row(peak), as_row(den))

    pl.semaphore_wait(barrier, n_dp - 1 + n_ex - 1)
    dp_far = list(range(n_dp - 1, 0, -1))
    ex_far = list(range(n_ex - 1, 0, -1))
    stat_copies = launch(
        [to_dp(stat1, rstat1.at[i], ss1.at[i], rs1.at[i], i) for i in dp_far]
    )
    weights = wts[...]
    num_copies = {}
    for i in dp_far + [0]:
        num1[i] = jnp.dot(
            weights, tok[:, strip(dp_to[i])], preferred_element_type=F32
        ).astype(BF16)
        if i:
            num_copies[i] = to_dp(num1.at[i], rnum1.at[i], sn1.at[i], rn1.at[i], i)
            num_copies[i].start()

    for copy in stat_copies:
        copy.wait_recv()

    def join(stats):
        high = stats[0][0:1]
        for stat in stats[1:]:
            high = jnp.maximum(high, stat[0:1])
        low = stats[0][1:2] * jnp.exp(stats[0][0:1] - high)
        for stat in stats[1:]:
            low = low + stat[1:2] * jnp.exp(stat[0:1] - high)
        return high, low

    stats = [stat1[...]] + [rstat1[i] for i in range(1, n_dp)]
    high, low = join(stats)
    stat2[...] = jnp.where(stat_row == 0, high, low)
    stat2_copies = launch(
        [to_ex(stat2, rstat2.at[i], ss2.at[i], rs2.at[i], i) for i in ex_far]
    )

    raw = logits[...]
    risen = jnp.exp(raw - jnp.max(raw, axis=0, keepdims=True))
    mix[...] = (risen / jnp.sum(risen, axis=0, keepdims=True)).T.astype(BF16)

    for copy in stat2_copies:
        copy.wait_recv()
    high, low = join([stat2[...]] + [rstat2[i] for i in range(1, n_ex)])
    scales = [as_column(jnp.exp(stat[0:1] - high) / low) for stat in stats]
    joint = scales[0] * num1[0].astype(F32)
    for i in range(1, n_dp):
        num_copies[i].wait_recv()
        joint = joint + scales[i] * rnum1[i].astype(F32)
    joint = joint.reshape(n_ex, per_dev, cols)
    if folded:
        joint = jnp.concatenate([joint[:, :, :cols // 2], joint[:, :, cols // 2:]], axis=1)
    send2[...] = joint.astype(send2.dtype)

    copies2 = launch(
        [to_ex(send2.at[ex_to[i]], recv2.at[i], s2.at[i], r2.at[i], i) for i in ex_far]
    )
    value = send2[k].astype(F32)
    for copy in copies2:
        copy.wait_recv()
    for i in range(1, n_ex):
        value = value + recv2[i].astype(F32)
    xs[...] = value.astype(BF16).astype(xs.dtype)

    copies3 = launch([to_dp(xs, rx.at[i], s3.at[i], r3.at[i], i) for i in range(1, n_dp)])
    for load in load_in:
        load.wait()
    sums = [jnp.zeros((per_dev, hid), F32) for _ in range(exp_dev)]
    for i in range(n_dp):
        if i:
            copies3[i - 1].wait_recv()
        x = rx[i] if i else xs[...]
        x = (unfold(x) if folded else x).astype(BF16)
        start = pl.multiple_of(dp_from[i] * cols, cols)
        for e in range(exp_dev):
            sums[e] = sums[e] + jnp.dot(
                x, win[e, pl.ds(start, cols), :], preferred_element_type=F32
            )
    hidden = [gelu(s).astype(BF16) for s in sums]
    for load in load_out:
        load.wait()
    own_slots = per_dev // exp_dev
    owner = lax.broadcasted_iota(jnp.int32, (per_dev, cols), 0) // own_slots
    copies4 = {}
    for i in dp_far + [0]:
        value = jnp.zeros((per_dev, cols), F32)
        for e in range(exp_dev):
            made = jnp.dot(hidden[e], wout[e, :, strip(dp_to[i])], preferred_element_type=F32)
            value = jnp.where(owner == e, made, value)
        part[i] = value
        if i:
            copies4[i] = to_dp(part.at[i], rpart.at[i], s4.at[i], r4.at[i], i)
            copies4[i].start()
    value = part[0]
    for i in range(1, n_dp):
        copies4[i].wait_recv()
        value = value + rpart[i]

    own5[...] = fold(value) if folded else value.astype(BF16).astype(F32)
    copies5 = launch(
        [to_ex(own5, recv5.at[i], s5.at[i], r5.at[i], i) for i in range(1, n_ex)]
    )
    copies6 = {}
    for b in range(n_ex):
        if b:
            copies5[b - 1].wait_recv()
        block_ref = recv5.at[b] if b else own5
        for i in dp_far:
            copies6[i, b] = to_dp(block_ref, recv6.at[i, b], s6.at[i, b], r6.at[i, b], i)
            copies6[i, b].start()
    for copy in copies2:
        copy.wait_send()
    mixing = mix[...]
    for i in range(n_dp):
        for b in range(n_ex):
            if i:
                copies6[i, b].wait_recv()
            item = recv6[i, b] if i else (recv5[b] if b else own5[...])
            send2[ex_from[b]] = item
        table = send2[...].astype(F32)
        if folded:
            table = jnp.concatenate([table[:, :per_dev, :], table[:, per_dev:, :]], axis=2)
        table = table.reshape(slots, cols).astype(BF16)
        out_ref[:, strip(dp_from[i])] = jnp.dot(
            mixing, table, preferred_element_type=F32
        ).astype(BF16)
    for copy in (
        stat_copies + list(num_copies.values()) + stat2_copies + copies3
        + list(copies4.values()) + copies5 + list(copies6.values())
    ):
        copy.wait_send()


def local(n_dp, n_ex, tokens, slot_param, pattern, w_in, w_out):
    rows, width = tokens.shape
    slots = slot_param.shape[1]
    cols = width // n_dp
    per_dev = slots // n_ex
    lanes = -(-slots // 128) * 128
    pieces = 4
    item = ((2 * per_dev, cols // 2), BF16) if cols % 256 == 0 else ((per_dev, cols), F32)
    dma = pltpu.SemaphoreType.DMA
    vmem, in_hbm = pl.BlockSpec(memory_space=pltpu.VMEM), pl.BlockSpec(memory_space=pltpu.HBM)
    operands = (tokens, slot_param.T, pattern.T, w_in, w_out)
    placed = [pltpu.with_memory_space_constraint(x, pltpu.HBM) for x in operands]
    return pl.pallas_call(
        functools.partial(slots_kernel, n_dp, n_ex, pieces),
        out_shape=jax.ShapeDtypeStruct((rows, width), BF16),
        in_specs=[in_hbm] * 5,
        out_specs=vmem,
        scratch_shapes=[
            pltpu.VMEM((slots, width), BF16),
            pltpu.VMEM(pattern.shape[::-1], pattern.dtype),
            pltpu.VMEM((rows, width), BF16),
            pltpu.VMEM(w_in.shape, BF16),
            pltpu.VMEM(w_out.shape, BF16),
            pltpu.VMEM((slots, rows), F32),
            pltpu.VMEM((slots, rows), BF16),
            pltpu.VMEM((rows, slots), BF16),
            pltpu.VMEM((8, lanes), F32),
            pltpu.VMEM((n_dp, 8, lanes), F32),
            pltpu.VMEM((n_dp, slots, cols), BF16),
            pltpu.VMEM((n_dp, slots, cols), BF16),
            pltpu.VMEM((8, lanes), F32),
            pltpu.VMEM((n_ex, 8, lanes), F32),
            pltpu.VMEM((n_ex,) + item[0], item[1]),
            pltpu.VMEM((n_ex,) + item[0], item[1]),
            pltpu.VMEM(*item),
            pltpu.VMEM((n_dp,) + item[0], item[1]),
            pltpu.VMEM((n_dp, per_dev, cols), F32),
            pltpu.VMEM((n_dp, per_dev, cols), F32),
            pltpu.VMEM(*item),
            pltpu.VMEM((n_ex,) + item[0], item[1]),
            pltpu.VMEM((n_dp, n_ex) + item[0], item[1]),
            dma((pieces,)),
            dma((4 * w_in.shape[0],)),
            dma((2,)),
        ]
        + [
            dma(shape)
            for shape in (
                (n_dp,), (n_dp,), (n_ex,), (n_ex,), (n_dp,), (n_dp,), (n_ex,), (n_dp, n_ex)
            )
            for _ in range(2)
        ],
        compiler_params=pltpu.CompilerParams(
            collective_id=0, has_side_effects=True, vmem_limit_bytes=48 * 1024 * 1024
        ),
        cost_estimate=pl.CostEstimate(
            flops=6 * rows * width * slots + 4 * per_dev * w_in.size // w_in.shape[0],
            bytes_accessed=2 * (tokens.size + w_in.size + w_out.size),
            transcendentals=2 * rows * slots,
        ),
    )(*placed)


def solution(mesh):
    return jax.shard_map(
        functools.partial(local, mesh.shape["dp"], mesh.shape["expert"]),
        mesh=mesh,
        in_specs=(
            P(("dp", "expert"), None),
            P(),
            P(None, ("dp", "expert")),
            P("expert", None, "dp"),
            P("expert", "dp", None),
        ),
        out_specs=P(("dp", "expert"), None),
        check_vma=False,
    )
```

```python
import functools

import jax
import jax.numpy as jnp
from jax import lax
from jax.experimental import pallas as pl
from jax.experimental.pallas import tpu as pltpu
from jax.sharding import PartitionSpec as P

MESH = pl.DeviceIdType.MESH
floor_value = -1e30
F32, BF16 = jnp.float32, jnp.bfloat16


def nt_dot(a, b):
    return lax.dot_general(a, b, (((1,), (1,)), ((), ())), preferred_element_type=F32)


def gelu(x):
    return 0.5 * x * (1.0 + jnp.tanh(0.7978845608028654 * (x + 0.044715 * (x * x * x))))


def fold(x):
    half = x.shape[-1] // 2
    return jnp.concatenate([x[..., :half], x[..., half:]], axis=x.ndim - 2)


def unfold(x):
    rows = x.shape[-2] // 2
    return jnp.concatenate([x[..., :rows, :], x[..., rows:, :]], axis=x.ndim - 1)


def flip(me, i, n):
    if n & (n - 1):
        return lax.rem(me + i, n), lax.rem(me + n - i, n)
    other, bit = 0, 1
    while bit < n:
        own = lax.rem(me // bit, 2)
        other = other + bit * ((1 - own) if i & bit else own)
        bit *= 2
    return other, other


def slots_kernel(
    n_dp, n_ex, pieces, strips,
    tok_hbm, slot_hbm, pat_hbm, win_hbm, wout_hbm,
    out_ref,
    slot_ref, pat_ref, tok, win, wout, logits, wts, mix, stat1, rstat1, stat2, rstat2, stat3, rstat3,
    num1, rnum1, send2, recv2, send3, recv3, part, rpart, own5, recv5, recv6, tab,
    tok_sem, w_sem, a_sem,
    ss1, rs1, ss2, rs2, ss3, rs3, s1, r1, s2, r2, s3, r3, s4, r4, s5, r5, s6, r6,
):
    d, k = lax.axis_index("dp"), lax.axis_index("expert")
    n_z = n_ex // 2
    z, c = k // 2, lax.rem(k, 2)
    slots, width = slot_ref.shape
    rows = tok.shape[0]
    cols = width // strips
    per_dev = slots // n_ex
    exp_dev, _, hid = win.shape
    blocks = pat_ref.shape[0]
    block = rows // blocks
    lanes = stat1.shape[1]
    piece = rows // pieces
    dp_to, _ = zip(*[flip(d, i, n_dp) for i in range(n_dp)])
    z_to, z_from = zip(*[flip(z, i, n_z) for i in range(n_z)])
    dp_far = list(range(n_dp - 1, 0, -1))
    z_far = list(range(n_z - 1, 0, -1))
    other = {"expert": 2 * z + 1 - c}
    dp_ids = [{"dp": target} for target in dp_to]
    z_ids = [{"expert": 2 * target + c} for target in z_to]

    def to(target, src, dst, ssem, rsem):
        return pltpu.make_async_remote_copy(
            src_ref=src, dst_ref=dst, send_sem=ssem, recv_sem=rsem,
            device_id=target, device_id_type=MESH,
        )

    sent = []

    def launch(copies):
        for copy in copies:
            copy.start()
        return copies

    def send(copies):
        sent.extend(copies)
        return launch(copies)

    def arrive(copies):
        for copy in copies:
            copy.wait_recv()

    loads = [
        pltpu.make_async_copy(
            tok_hbm.at[pl.ds(p * piece, piece)], tok.at[pl.ds(p * piece, piece)], tok_sem.at[p]
        )
        for p in range(pieces)
    ]
    load_slot = pltpu.make_async_copy(slot_hbm, slot_ref, a_sem.at[0])
    load_pat = pltpu.make_async_copy(pat_hbm, pat_ref, a_sem.at[1])
    launch([load_slot, load_pat] + loads)
    barrier = pltpu.get_barrier_semaphore()
    for target in [other] + dp_ids[1:] + z_ids[1:]:
        pl.semaphore_signal(barrier, inc=1, device_id=target, device_id_type=MESH)

    def in_parts(src, dst, first):
        depth = src.shape[1] // 2
        return [
            pltpu.make_async_copy(
                src.at[e, pl.ds(h * depth, depth)], dst.at[e, pl.ds(h * depth, depth)],
                w_sem.at[first + 2 * e + h],
            )
            for e in range(exp_dev) for h in range(2)
        ]

    load_in = in_parts(win_hbm, win, 0)
    load_out = in_parts(wout_hbm, wout, 2 * exp_dev)

    row_id = lax.broadcasted_iota(jnp.int32, (slots, lanes), 0)
    lane_id = lax.broadcasted_iota(jnp.int32, (slots, lanes), 1)
    eye = row_id == lane_id

    def as_column(row):
        return jnp.sum(jnp.where(eye, row, 0.0), axis=1, keepdims=True)

    own_shape = (2 * per_dev, lanes)
    own_row = lax.rem(lax.broadcasted_iota(jnp.int32, own_shape, 0), per_dev) + k * per_dev
    own_eye = own_row == lax.broadcasted_iota(jnp.int32, own_shape, 1)

    def own_column(row):
        return jnp.sum(jnp.where(own_eye, row, 0.0), axis=1, keepdims=True)

    def of_core(x):
        x = x.reshape(n_z, 2, per_dev, x.shape[-1])
        return jnp.where(c == 0, x[:, 0], x[:, 1]).reshape(n_z * per_dev, x.shape[-1])

    def as_row(column):
        return jnp.sum(jnp.where(eye, column, 0.0), axis=0, keepdims=True)

    load_slot.wait()
    load_pat.wait()
    slot_t = slot_ref[...]
    for p in range(pieces):
        loads[p].wait()
        if p == pieces - 1:
            launch(load_in + load_out)
        span = slice(p * piece, (p + 1) * piece)
        logits[:, span] = nt_dot(tok[span, :], slot_t).T

    seen = pat_ref[...].astype(F32)
    if lanes > slots:
        seen = jnp.concatenate([seen, jnp.zeros((blocks, lanes - slots), F32)], axis=1)
    columns = [as_column(seen[b:b + 1, :]) > 0.0 for b in range(blocks)]
    masked = [
        jnp.where(columns[b], logits[:, b * block:(b + 1) * block], floor_value)
        for b in range(blocks)
    ]
    top = masked[0]
    for b in range(1, blocks):
        top = jnp.maximum(top, masked[b])
    peak = jnp.max(top, axis=1, keepdims=True)
    total = jnp.zeros((slots, block), F32)
    for b in range(blocks):
        shifted = jnp.where(columns[b], masked[b] - peak, floor_value)
        weight = jnp.exp(shifted).astype(BF16)
        wts[:, b * block:(b + 1) * block] = weight
        total = total + weight.astype(F32)
    den = jnp.sum(total, axis=1, keepdims=True)
    stat_row = lax.broadcasted_iota(jnp.int32, stat1.shape, 0)
    stat1[...] = jnp.where(stat_row == 0, as_row(peak), as_row(den))

    def join(stats):
        high = stats[0][0:1]
        for stat in stats[1:]:
            high = jnp.maximum(high, stat[0:1])
        scales = [jnp.exp(stat[0:1] - high) for stat in stats]
        low = stats[0][1:2] * scales[0]
        for stat, scale in zip(stats[1:], scales[1:]):
            low = low + stat[1:2] * scale
        return high, low, scales

    pl.semaphore_wait(barrier, n_dp - 1 + n_z)
    stat_copy = send([to(other, stat1, rstat1, ss1, rs1)])
    weights = wts[...]
    copies1, copies2, copies3 = {}, {}, {}

    def numerator(j):
        made = jnp.dot(weights, tok[:, j * cols:(j + 1) * cols], preferred_element_type=F32)
        made = made.astype(BF16).astype(F32).reshape(n_z, 2, per_dev, cols)
        for side in range(2):
            num1[j, side] = made[:, side].reshape(n_z * per_dev, cols).astype(BF16)
        copies1[j] = send([to(other, num1.at[j, 1 - c], rnum1.at[j], s1.at[j], r1.at[j])])

    def over_core(j):
        arrive(copies1[j])
        joint = mine * num1[j, c].astype(F32) + theirs * rnum1[j].astype(F32)
        send2[j] = fold(joint.reshape(n_z, per_dev, cols)).astype(BF16)
        copies2[j] = send([
            to(z_ids[i], send2.at[j, z_to[i]], recv2.at[j, i], s2.at[j, i], r2.at[j, i])
            for i in z_far
        ])

    def over_z(j):
        arrive(copies2[j])
        value = z_scales[0] * send2[j, z].astype(F32)
        for i in range(1, n_z):
            value = value + z_scales[i] * recv2[j, i].astype(F32)
        send3[j] = value.astype(BF16)
        copies3[j] = send([
            to(dp_ids[i], send3.at[j], recv3.at[j, i], s3.at[j, i], r3.at[j, i]) for i in dp_far
        ])

    numerator(0)
    numerator(1)
    arrive(stat_copy)
    high, low, scales = join([stat1[...], rstat1[...]])
    stat2[...] = jnp.where(stat_row == 0, high, low)
    stat2_copies = send([
        to(z_ids[i], stat2, rstat2.at[i], ss2.at[i], rs2.at[i]) for i in z_far
    ])
    mine, theirs = [of_core(as_column(scale)) for scale in scales]
    over_core(0)
    for j in range(2, strips):
        numerator(j)
        over_core(j - 1)
    over_core(strips - 1)

    raw = logits[...]
    risen = jnp.exp(raw - jnp.max(raw, axis=0, keepdims=True))
    mix[...] = (risen / jnp.sum(risen, axis=0, keepdims=True)).T.astype(BF16)

    arrive(stat2_copies)
    high, low, scales = join([stat2[...]] + [rstat2[i] for i in range(1, n_z)])
    stat3[...] = jnp.where(stat_row == 0, high, low)
    stat3_copies = send([
        to(dp_ids[i], stat3, rstat3.at[i], ss3.at[i], rs3.at[i]) for i in dp_far
    ])
    z_scales = [own_column(scale) for scale in scales]
    for j in range(strips):
        over_z(j)
    arrive(stat3_copies)
    high, low, scales = join([stat3[...]] + [rstat3[i] for i in range(1, n_dp)])
    dp_scales = [own_column(scale / low) for scale in scales]
    for load in load_in:
        load.wait()
    sums = [jnp.zeros((per_dev, hid), F32) for _ in range(exp_dev)]
    for j in range(strips):
        arrive(copies3[j])
        value = dp_scales[0] * send3[j].astype(F32)
        for i in range(1, n_dp):
            value = value + dp_scales[i] * recv3[j, i].astype(F32)
        x = unfold(value).astype(BF16)
        for e in range(exp_dev):
            sums[e] = sums[e] + jnp.dot(
                x, win[e, j * cols:(j + 1) * cols, :], preferred_element_type=F32
            )

    hidden = [gelu(total).astype(BF16) for total in sums]
    for load in load_out:
        load.wait()
    own_slots = per_dev // exp_dev
    owner = lax.broadcasted_iota(jnp.int32, (per_dev, cols), 0) // own_slots
    copies4, copies5, copies6 = {}, {}, {}
    for j in range(strips):
        value = jnp.zeros((per_dev, cols), F32)
        for e in range(exp_dev):
            made = jnp.dot(
                hidden[e], wout[e, :, j * cols:(j + 1) * cols], preferred_element_type=F32
            )
            value = jnp.where(owner == e, made, value)
        part[j] = fold(value).astype(BF16)
        copies4[j] = send([
            to(dp_ids[i], part.at[j], rpart.at[j, i], s4.at[j, i], r4.at[j, i]) for i in dp_far
        ])

    def to_core(src, j, i):
        copies6[j, i] = send([to(other, src, recv6.at[j, i], s6.at[j, i], r6.at[j, i])])

    for j in range(strips):
        arrive(copies4[j])
        value = part[j].astype(F32)
        for i in range(1, n_dp):
            value = value + rpart[j, i].astype(F32)
        own5[j] = value.astype(BF16)
        copies5[j] = {
            i: send([to(z_ids[i], own5.at[j], recv5.at[j, i], s5.at[j, i], r5.at[j, i])])
            for i in z_far
        }
        to_core(own5.at[j], j, 0)
    mixing = mix[...]

    def pass_on(j):
        for i in range(1, n_z):
            arrive(copies5[j][i])
            to_core(recv5.at[j, i], j, i)

    def mixed(j):
        for i in range(n_z):
            arrive(copies6[j, i])
            tab[z_from[i], c] = recv5[j, i] if i else own5[j]
            tab[z_from[i], 1 - c] = recv6[j, i]
        table = unfold(tab[...].astype(F32).reshape(n_ex, 2 * per_dev, cols // 2))
        table = table.reshape(slots, cols).astype(BF16)
        out_ref[:, j * cols:(j + 1) * cols] = jnp.dot(
            mixing, table, preferred_element_type=F32
        ).astype(BF16)

    pass_on(0)
    for j in range(1, strips):
        pass_on(j)
        mixed(j - 1)
    mixed(strips - 1)
    for copy in sent:
        copy.wait_send()


def local(n_dp, n_ex, tokens, slot_param, pattern, w_in, w_out):
    rows, width = tokens.shape
    slots = slot_param.shape[1]
    per_dev = slots // n_ex
    lanes = -(-slots // 128) * 128
    n_z = n_ex // 2
    pieces, strips = 4, 4
    cols = width // strips
    flat = (2 * per_dev, cols // 2)
    dma = pltpu.SemaphoreType.DMA
    in_hbm = pl.BlockSpec(memory_space=pltpu.HBM)
    operands = (tokens, slot_param.T, pattern.T, w_in, w_out)
    placed = [pltpu.with_memory_space_constraint(x, pltpu.HBM) for x in operands]
    scratch = [
        ((slots, width), BF16),
        (pattern.shape[::-1], pattern.dtype),
        ((rows, width), BF16),
        (w_in.shape, BF16),
        (w_out.shape, BF16),
        ((slots, rows), F32),
        ((slots, rows), BF16),
        ((rows, slots), BF16),
        ((8, lanes), F32),
        ((8, lanes), F32),
        ((8, lanes), F32),
        ((n_z, 8, lanes), F32),
        ((8, lanes), F32),
        ((n_dp, 8, lanes), F32),
        ((strips, 2, n_z * per_dev, cols), BF16),
        ((strips, n_z * per_dev, cols), BF16),
        ((strips, n_z) + flat, BF16),
        ((strips, n_z) + flat, BF16),
        ((strips,) + flat, BF16),
        ((strips, n_dp) + flat, BF16),
        ((strips,) + flat, BF16),
        ((strips, n_dp) + flat, BF16),
        ((strips,) + flat, BF16),
        ((strips, n_z) + flat, BF16),
        ((strips, n_z) + flat, BF16),
        ((n_z, 2) + flat, BF16),
    ]
    by_z, by_dp = (strips, n_z), (strips, n_dp)
    remote = [None, (n_z,), (n_dp,), (strips,), by_z, by_dp, by_dp, by_z, by_z]
    return pl.pallas_call(
        functools.partial(slots_kernel, n_dp, n_ex, pieces, strips),
        out_shape=jax.ShapeDtypeStruct((rows, width), BF16),
        in_specs=[in_hbm] * 5,
        out_specs=pl.BlockSpec(memory_space=pltpu.VMEM),
        scratch_shapes=[pltpu.VMEM(*one) for one in scratch]
        + [dma((pieces,)), dma((4 * w_in.shape[0],)), dma((2,))]
        + [dma(shape) if shape else dma for shape in remote for _ in range(2)],
        compiler_params=pltpu.CompilerParams(
            collective_id=0, has_side_effects=True, vmem_limit_bytes=48 * 1024 * 1024
        ),
        cost_estimate=pl.CostEstimate(
            flops=6 * rows * width * slots + 4 * per_dev * w_in.size // w_in.shape[0],
            bytes_accessed=2 * (tokens.size + w_in.size + w_out.size),
            transcendentals=2 * rows * slots,
        ),
    )(*placed)


def solution(mesh):
    return jax.shard_map(
        functools.partial(local, mesh.shape["dp"], mesh.shape["expert"]),
        mesh=mesh,
        in_specs=(
            P(("dp", "expert"), None),
            P(),
            P(None, ("dp", "expert")),
            P("expert", None, "dp"),
            P("expert", "dp", None),
        ),
        out_specs=P(("dp", "expert"), None),
        check_vma=False,
    )
```

```python
import functools

import jax
import jax.numpy as jnp
from jax import lax
from jax.experimental import pallas as pl
from jax.experimental.pallas import tpu as pltpu
from jax.sharding import PartitionSpec as P

MESH = pl.DeviceIdType.MESH
floor_value = -1e30
F32, BF16 = jnp.float32, jnp.bfloat16


def gelu(x):
    return 0.5 * x * (1.0 + jnp.tanh(0.7978845608028654 * (x + 0.044715 * (x * x * x))))


def fold(x):
    half = x.shape[-1] // 2
    return jnp.concatenate([x[..., :half], x[..., half:]], axis=x.ndim - 2)


def unfold(x):
    rows = x.shape[-2] // 2
    return jnp.concatenate([x[..., :rows, :], x[..., rows:, :]], axis=x.ndim - 1)


def flip(me, i, n):
    if n & (n - 1):
        return lax.rem(me + i, n), lax.rem(me + n - i, n)
    other, bit = 0, 1
    while bit < n:
        own = lax.rem(me // bit, 2)
        other = other + bit * ((1 - own) if i & bit else own)
        bit *= 2
    return other, other


def slots_kernel(
    n_dp, n_ex, pieces, strips,
    tok_hbm, slot_hbm, pat_hbm, win_hbm, wout_hbm,
    out_ref,
    slot_ref, slot_in, mask, pat_ref, tok, win, wout, logits, wts, mix, stat1, rstat1, stat2, rstat2, stat3, rstat3,
    num1, rnum1, send2, recv2, send3, recv3, part, rpart, own5, recv5, recv6, tab,
    tok_sem, w_sem, a_sem,
    ss1, rs1, ss2, rs2, ss3, rs3, s1, r1, s2, r2, s3, r3, s4, r4, s5, r5, s6, r6,
):
    d, k = lax.axis_index("dp"), lax.axis_index("expert")
    n_z = n_ex // 2
    z, c = k // 2, lax.rem(k, 2)
    slots, width = slot_ref.shape
    rows = tok.shape[0]
    cols = width // strips
    per_dev = slots // n_ex
    exp_dev, _, hid = win.shape
    blocks = pat_ref.shape[0]
    block = rows // blocks
    lanes = stat1.shape[1]
    piece = rows // pieces
    dp_to, _ = zip(*[flip(d, i, n_dp) for i in range(n_dp)])
    z_to, z_from = zip(*[flip(z, i, n_z) for i in range(n_z)])
    dp_far = list(range(n_dp - 1, 0, -1))
    z_far = list(range(n_z - 1, 0, -1))
    other = {"expert": 2 * z + 1 - c}
    dp_ids = [{"dp": target} for target in dp_to]
    z_ids = [{"expert": 2 * target + c} for target in z_to]

    def to(target, src, dst, ssem, rsem):
        return pltpu.make_async_remote_copy(
            src_ref=src, dst_ref=dst, send_sem=ssem, recv_sem=rsem,
            device_id=target, device_id_type=MESH,
        )

    sent = []

    def launch(copies):
        for copy in copies:
            copy.start()
        return copies

    def send(copies):
        sent.extend(copies)
        return launch(copies)

    def arrive(copies):
        for copy in copies:
            copy.wait_recv()

    loads = [
        pltpu.make_async_copy(
            tok_hbm.at[pl.ds(p * piece, piece)], tok.at[pl.ds(p * piece, piece)], tok_sem.at[p]
        )
        for p in range(pieces)
    ]
    load_slot = pltpu.make_async_copy(slot_hbm, slot_ref, a_sem.at[0])
    load_pat = pltpu.make_async_copy(pat_hbm, pat_ref, a_sem.at[1])
    launch([load_slot, load_pat] + loads)
    barrier = pltpu.get_barrier_semaphore()
    for target in [other] + dp_ids[1:] + z_ids[1:]:
        pl.semaphore_signal(barrier, inc=1, device_id=target, device_id_type=MESH)

    def in_parts(src, dst, first):
        depth = src.shape[1] // 2
        return [
            pltpu.make_async_copy(
                src.at[e, pl.ds(h * depth, depth)], dst.at[e, pl.ds(h * depth, depth)],
                w_sem.at[first + 2 * e + h],
            )
            for e in range(exp_dev) for h in range(2)
        ]

    load_in = in_parts(win_hbm, win, 0)
    load_out = in_parts(wout_hbm, wout, 2 * exp_dev)

    row_id = lax.broadcasted_iota(jnp.int32, (slots, lanes), 0)
    lane_id = lax.broadcasted_iota(jnp.int32, (slots, lanes), 1)
    eye = row_id == lane_id

    def as_column(row):
        return jnp.sum(jnp.where(eye, row, 0.0), axis=1, keepdims=True)

    own_shape = (2 * per_dev, lanes)
    own_row = lax.rem(lax.broadcasted_iota(jnp.int32, own_shape, 0), per_dev) + k * per_dev
    own_eye = own_row == lax.broadcasted_iota(jnp.int32, own_shape, 1)

    def own_column(row):
        return jnp.sum(jnp.where(own_eye, row, 0.0), axis=1, keepdims=True)

    def of_core(x):
        x = x.reshape(n_z, 2, per_dev, x.shape[-1])
        return jnp.where(c == 0, x[:, 0], x[:, 1]).reshape(n_z * per_dev, x.shape[-1])

    def as_row(column):
        return jnp.sum(jnp.where(eye, column, 0.0), axis=0, keepdims=True)

    load_slot.wait()
    load_pat.wait()
    slot_in[...] = slot_ref[...].astype(F32).T.astype(BF16)
    seen = pat_ref[...].astype(F32)
    if lanes > slots:
        seen = jnp.concatenate([seen, jnp.zeros((blocks, lanes - slots), F32)], axis=1)
    for b in range(blocks):
        mask[:, b * block:(b + 1) * block] = jnp.broadcast_to(
            as_column(seen[b:b + 1, :]), (slots, block)
        )

    top = jnp.full((slots, piece), floor_value, F32)
    for p in range(pieces):
        loads[p].wait()
        if p == pieces - 1:
            launch(load_in + load_out)
        span = slice(p * piece, (p + 1) * piece)
        made = jnp.dot(tok[span, :], slot_in[...], preferred_element_type=F32).T
        logits[:, span] = made
        top = jnp.maximum(top, jnp.where(mask[:, span] > 0.0, made, floor_value))
    peak = jnp.max(top, axis=1, keepdims=True)
    raw = logits[...]
    shifted = jnp.where(mask[...] > 0.0, raw - peak, floor_value)
    weights = jnp.exp(shifted).astype(BF16)
    wts[...] = weights
    den = jnp.sum(weights.astype(F32), axis=1, keepdims=True)
    stat_row = lax.broadcasted_iota(jnp.int32, stat1.shape, 0)
    stat1[...] = jnp.where(stat_row == 0, as_row(peak), as_row(den))

    def join(stats):
        high = stats[0][0:1]
        for stat in stats[1:]:
            high = jnp.maximum(high, stat[0:1])
        scales = [jnp.exp(stat[0:1] - high) for stat in stats]
        low = stats[0][1:2] * scales[0]
        for stat, scale in zip(stats[1:], scales[1:]):
            low = low + stat[1:2] * scale
        return high, low, scales

    pl.semaphore_wait(barrier, n_dp - 1 + n_z)
    stat_copy = send([to(other, stat1, rstat1, ss1, rs1)])
    weights = wts[...]
    copies1, copies2, copies3 = {}, {}, {}

    def numerator(j):
        made = jnp.dot(weights, tok[:, j * cols:(j + 1) * cols], preferred_element_type=F32)
        made = made.astype(BF16).astype(F32).reshape(n_z, 2, per_dev, cols)
        for side in range(2):
            num1[j, side] = made[:, side].reshape(n_z * per_dev, cols).astype(BF16)
        copies1[j] = send([to(other, num1.at[j, 1 - c], rnum1.at[j], s1.at[j], r1.at[j])])

    def over_core(j):
        arrive(copies1[j])
        joint = mine * num1[j, c].astype(F32) + theirs * rnum1[j].astype(F32)
        send2[j] = fold(joint.reshape(n_z, per_dev, cols)).astype(BF16)
        copies2[j] = send([
            to(z_ids[i], send2.at[j, z_to[i]], recv2.at[j, i], s2.at[j, i], r2.at[j, i])
            for i in z_far
        ])

    def over_z(j):
        arrive(copies2[j])
        value = z_scales[0] * send2[j, z].astype(F32)
        for i in range(1, n_z):
            value = value + z_scales[i] * recv2[j, i].astype(F32)
        send3[j] = value.astype(BF16)
        copies3[j] = send([
            to(dp_ids[i], send3.at[j], recv3.at[j, i], s3.at[j, i], r3.at[j, i]) for i in dp_far
        ])

    numerator(0)
    numerator(1)
    arrive(stat_copy)
    high, low, scales = join([stat1[...], rstat1[...]])
    stat2[...] = jnp.where(stat_row == 0, high, low)
    stat2_copies = send([
        to(z_ids[i], stat2, rstat2.at[i], ss2.at[i], rs2.at[i]) for i in z_far
    ])
    mine, theirs = [of_core(as_column(scale)) for scale in scales]
    over_core(0)
    for j in range(2, strips):
        numerator(j)
        over_core(j - 1)
    over_core(strips - 1)

    raw = logits[...]
    risen = jnp.exp(raw - jnp.max(raw, axis=0, keepdims=True))
    mix[...] = (risen / jnp.sum(risen, axis=0, keepdims=True)).T.astype(BF16)

    arrive(stat2_copies)
    high, low, scales = join([stat2[...]] + [rstat2[i] for i in range(1, n_z)])
    stat3[...] = jnp.where(stat_row == 0, high, low)
    stat3_copies = send([
        to(dp_ids[i], stat3, rstat3.at[i], ss3.at[i], rs3.at[i]) for i in dp_far
    ])
    z_scales = [own_column(scale) for scale in scales]
    for j in range(strips):
        over_z(j)
    arrive(stat3_copies)
    high, low, scales = join([stat3[...]] + [rstat3[i] for i in range(1, n_dp)])
    dp_scales = [own_column(scale / low) for scale in scales]
    for load in load_in:
        load.wait()
    sums = [jnp.zeros((per_dev, hid), F32) for _ in range(exp_dev)]
    for j in range(strips):
        arrive(copies3[j])
        value = dp_scales[0] * send3[j].astype(F32)
        for i in range(1, n_dp):
            value = value + dp_scales[i] * recv3[j, i].astype(F32)
        x = unfold(value).astype(BF16)
        for e in range(exp_dev):
            sums[e] = sums[e] + jnp.dot(
                x, win[e, j * cols:(j + 1) * cols, :], preferred_element_type=F32
            )

    hidden = [gelu(total).astype(BF16) for total in sums]
    for load in load_out:
        load.wait()
    own_slots = per_dev // exp_dev
    owner = lax.broadcasted_iota(jnp.int32, (per_dev, cols), 0) // own_slots
    copies4, copies5, copies6 = {}, {}, {}
    for j in range(strips):
        value = jnp.zeros((per_dev, cols), F32)
        for e in range(exp_dev):
            made = jnp.dot(
                hidden[e], wout[e, :, j * cols:(j + 1) * cols], preferred_element_type=F32
            )
            value = jnp.where(owner == e, made, value)
        part[j] = fold(value).astype(BF16)
        copies4[j] = send([
            to(dp_ids[i], part.at[j], rpart.at[j, i], s4.at[j, i], r4.at[j, i]) for i in dp_far
        ])

    def to_core(src, j, i):
        copies6[j, i] = send([to(other, src, recv6.at[j, i], s6.at[j, i], r6.at[j, i])])

    for j in range(strips):
        arrive(copies4[j])
        value = part[j].astype(F32)
        for i in range(1, n_dp):
            value = value + rpart[j, i].astype(F32)
        own5[j] = value.astype(BF16)
        copies5[j] = {
            i: send([to(z_ids[i], own5.at[j], recv5.at[j, i], s5.at[j, i], r5.at[j, i])])
            for i in z_far
        }
        to_core(own5.at[j], j, 0)
    mixing = mix[...]

    def pass_on(j):
        for i in range(1, n_z):
            arrive(copies5[j][i])
            to_core(recv5.at[j, i], j, i)

    def mixed(j):
        for i in range(n_z):
            arrive(copies6[j, i])
            tab[z_from[i], c] = recv5[j, i] if i else own5[j]
            tab[z_from[i], 1 - c] = recv6[j, i]
        table = unfold(tab[...].astype(F32).reshape(n_ex, 2 * per_dev, cols // 2))
        table = table.reshape(slots, cols).astype(BF16)
        out_ref[:, j * cols:(j + 1) * cols] = jnp.dot(
            mixing, table, preferred_element_type=F32
        ).astype(BF16)

    pass_on(0)
    for j in range(1, strips):
        pass_on(j)
        mixed(j - 1)
    mixed(strips - 1)
    for copy in sent:
        copy.wait_send()


def local(n_dp, n_ex, tokens, slot_param, pattern, w_in, w_out):
    rows, width = tokens.shape
    slots = slot_param.shape[1]
    per_dev = slots // n_ex
    lanes = -(-slots // 128) * 128
    n_z = n_ex // 2
    pieces, strips = 4, 4
    cols = width // strips
    flat = (2 * per_dev, cols // 2)
    dma = pltpu.SemaphoreType.DMA
    in_hbm = pl.BlockSpec(memory_space=pltpu.HBM)
    operands = (tokens, slot_param.T, pattern.T, w_in, w_out)
    placed = [pltpu.with_memory_space_constraint(x, pltpu.HBM) for x in operands]
    scratch = [
        ((slots, width), BF16),
        ((width, slots), BF16),
        ((slots, rows), F32),
        (pattern.shape[::-1], pattern.dtype),
        ((rows, width), BF16),
        (w_in.shape, BF16),
        (w_out.shape, BF16),
        ((slots, rows), F32),
        ((slots, rows), BF16),
        ((rows, slots), BF16),
        ((8, lanes), F32),
        ((8, lanes), F32),
        ((8, lanes), F32),
        ((n_z, 8, lanes), F32),
        ((8, lanes), F32),
        ((n_dp, 8, lanes), F32),
        ((strips, 2, n_z * per_dev, cols), BF16),
        ((strips, n_z * per_dev, cols), BF16),
        ((strips, n_z) + flat, BF16),
        ((strips, n_z) + flat, BF16),
        ((strips,) + flat, BF16),
        ((strips, n_dp) + flat, BF16),
        ((strips,) + flat, BF16),
        ((strips, n_dp) + flat, BF16),
        ((strips,) + flat, BF16),
        ((strips, n_z) + flat, BF16),
        ((strips, n_z) + flat, BF16),
        ((n_z, 2) + flat, BF16),
    ]
    by_z, by_dp = (strips, n_z), (strips, n_dp)
    remote = [None, (n_z,), (n_dp,), (strips,), by_z, by_dp, by_dp, by_z, by_z]
    return pl.pallas_call(
        functools.partial(slots_kernel, n_dp, n_ex, pieces, strips),
        out_shape=jax.ShapeDtypeStruct((rows, width), BF16),
        in_specs=[in_hbm] * 5,
        out_specs=pl.BlockSpec(memory_space=pltpu.VMEM),
        scratch_shapes=[pltpu.VMEM(*one) for one in scratch]
        + [dma((pieces,)), dma((4 * w_in.shape[0],)), dma((2,))]
        + [dma(shape) if shape else dma for shape in remote for _ in range(2)],
        compiler_params=pltpu.CompilerParams(
            collective_id=0, has_side_effects=True, vmem_limit_bytes=48 * 1024 * 1024
        ),
        cost_estimate=pl.CostEstimate(
            flops=6 * rows * width * slots + 4 * per_dev * w_in.size // w_in.shape[0],
            bytes_accessed=2 * (tokens.size + w_in.size + w_out.size),
            transcendentals=2 * rows * slots,
        ),
    )(*placed)


def solution(mesh):
    return jax.shard_map(
        functools.partial(local, mesh.shape["dp"], mesh.shape["expert"]),
        mesh=mesh,
        in_specs=(
            P(("dp", "expert"), None),
            P(),
            P(None, ("dp", "expert")),
            P("expert", None, "dp"),
            P("expert", "dp", None),
        ),
        out_specs=P(("dp", "expert"), None),
        check_vma=False,
    )
```

```python
import functools

import jax
import jax.numpy as jnp
from jax import lax
from jax.experimental import pallas as pl
from jax.experimental.pallas import tpu as pltpu
from jax.sharding import PartitionSpec as P

MESH = pl.DeviceIdType.MESH
floor_value = -1e30
F32, BF16 = jnp.float32, jnp.bfloat16


def gelu(x):
    return 0.5 * x * (1.0 + jnp.tanh(0.7978845608028654 * (x + 0.044715 * (x * x * x))))


def fold(x):
    half = x.shape[-1] // 2
    return jnp.concatenate([x[..., :half], x[..., half:]], axis=x.ndim - 2)


def unfold(x):
    rows = x.shape[-2] // 2
    return jnp.concatenate([x[..., :rows, :], x[..., rows:, :]], axis=x.ndim - 1)


def flip(me, i, n):
    if n & (n - 1):
        return lax.rem(me + i, n), lax.rem(me + n - i, n)
    other, bit = 0, 1
    while bit < n:
        own = lax.rem(me // bit, 2)
        other = other + bit * ((1 - own) if i & bit else own)
        bit *= 2
    return other, other


def slots_kernel(
    n_dp, n_ex, pieces, strips,
    tok_hbm, slot_hbm, pat_hbm, win_hbm, wout_hbm,
    out_ref,
    slot_ref, slot_in, mask, pat_ref, tok, win, wout, logits, wts, mix, stat1, rstat1, stat2, rstat2, stat3, rstat3,
    num1, rnum1, send2, recv2, send3, recv3, part, rpart, own5, recv5, recv6, tab,
    tok_sem, w_sem, a_sem,
    ss1, rs1, ss2, rs2, ss3, rs3, s1, r1, s2, r2, s3, r3, s4, r4, s5, r5, s6, r6,
):
    d, k = lax.axis_index("dp"), lax.axis_index("expert")
    n_z = n_ex // 2
    z, c = k // 2, lax.rem(k, 2)
    slots, width = slot_ref.shape
    rows = tok.shape[0]
    cols = width // strips
    per_dev = slots // n_ex
    exp_dev, _, hid = win.shape
    blocks = pat_ref.shape[0]
    block = rows // blocks
    lanes = stat1.shape[1]
    piece = rows // pieces
    dp_to, _ = zip(*[flip(d, i, n_dp) for i in range(n_dp)])
    z_to, z_from = zip(*[flip(z, i, n_z) for i in range(n_z)])
    dp_far = list(range(n_dp - 1, 0, -1))
    z_far = list(range(n_z - 1, 0, -1))
    other = {"expert": 2 * z + 1 - c}
    dp_ids = [{"dp": target} for target in dp_to]
    z_ids = [{"expert": 2 * target + c} for target in z_to]

    def to(target, src, dst, ssem, rsem):
        return pltpu.make_async_remote_copy(
            src_ref=src, dst_ref=dst, send_sem=ssem, recv_sem=rsem,
            device_id=target, device_id_type=MESH,
        )

    sent = []

    def launch(copies):
        for copy in copies:
            copy.start()
        return copies

    def send(copies):
        sent.extend(copies)
        return launch(copies)

    def arrive(copies):
        for copy in copies:
            copy.wait_recv()

    def arrive_all(landed, sem):
        pltpu.make_async_copy(landed, landed, sem).wait()

    def drain():
        while sent:
            sent.pop(0).wait_send()

    loads = [
        pltpu.make_async_copy(
            tok_hbm.at[pl.ds(p * piece, piece)], tok.at[pl.ds(p * piece, piece)], tok_sem.at[p]
        )
        for p in range(pieces)
    ]
    load_slot = pltpu.make_async_copy(slot_hbm, slot_ref, a_sem.at[0])
    load_pat = pltpu.make_async_copy(pat_hbm, pat_ref, a_sem.at[1])
    launch([load_slot, load_pat] + loads)
    barrier = pltpu.get_barrier_semaphore()
    for target in [other] + dp_ids[1:] + z_ids[1:]:
        pl.semaphore_signal(barrier, inc=1, device_id=target, device_id_type=MESH)

    def in_parts(src, dst, first):
        depth = src.shape[1] // 2
        return [
            pltpu.make_async_copy(
                src.at[e, pl.ds(h * depth, depth)], dst.at[e, pl.ds(h * depth, depth)],
                w_sem.at[first + 2 * e + h],
            )
            for e in range(exp_dev) for h in range(2)
        ]

    load_in = in_parts(win_hbm, win, 0)
    load_out = in_parts(wout_hbm, wout, 2 * exp_dev)

    row_id = lax.broadcasted_iota(jnp.int32, (slots, lanes), 0)
    lane_id = lax.broadcasted_iota(jnp.int32, (slots, lanes), 1)
    eye = row_id == lane_id

    def as_column(row):
        return jnp.sum(jnp.where(eye, row, 0.0), axis=1, keepdims=True)

    own_shape = (2 * per_dev, lanes)
    own_row = lax.rem(lax.broadcasted_iota(jnp.int32, own_shape, 0), per_dev) + k * per_dev
    own_eye = own_row == lax.broadcasted_iota(jnp.int32, own_shape, 1)

    def own_column(row):
        return jnp.sum(jnp.where(own_eye, row, 0.0), axis=1, keepdims=True)

    def of_core(x):
        x = x.reshape(n_z, 2, per_dev, x.shape[-1])
        return jnp.where(c == 0, x[:, 0], x[:, 1]).reshape(n_z * per_dev, x.shape[-1])

    def as_row(column):
        return jnp.sum(jnp.where(eye, column, 0.0), axis=0, keepdims=True)

    load_slot.wait()
    load_pat.wait()
    slot_in[...] = slot_ref[...].astype(F32).T.astype(BF16)
    seen = pat_ref[...].astype(F32)
    if lanes > slots:
        seen = jnp.concatenate([seen, jnp.zeros((blocks, lanes - slots), F32)], axis=1)
    for b in range(blocks):
        mask[:, b * block:(b + 1) * block] = jnp.broadcast_to(
            as_column(seen[b:b + 1, :]), (slots, block)
        )

    top = jnp.full((slots, piece), floor_value, F32)
    for p in range(pieces):
        loads[p].wait()
        if p == pieces - 1:
            launch(load_in + load_out)
        span = slice(p * piece, (p + 1) * piece)
        made = jnp.dot(tok[span, :], slot_in[...], preferred_element_type=F32).T
        logits[:, span] = made
        top = jnp.maximum(top, jnp.where(mask[:, span] > 0.0, made, floor_value))
    peak = jnp.max(top, axis=1, keepdims=True)
    raw = logits[...]
    shifted = jnp.where(mask[...] > 0.0, raw - peak, floor_value)
    weights = jnp.exp(shifted).astype(BF16)
    wts[...] = weights
    den = jnp.sum(weights.astype(F32), axis=1, keepdims=True)
    stat_row = lax.broadcasted_iota(jnp.int32, stat1.shape, 0)
    stat1[...] = jnp.where(stat_row == 0, as_row(peak), as_row(den))

    def join(stats):
        high = stats[0][0:1]
        for stat in stats[1:]:
            high = jnp.maximum(high, stat[0:1])
        scales = [jnp.exp(stat[0:1] - high) for stat in stats]
        low = stats[0][1:2] * scales[0]
        for stat, scale in zip(stats[1:], scales[1:]):
            low = low + stat[1:2] * scale
        return high, low, scales

    pl.semaphore_wait(barrier, n_dp - 1 + n_z)
    stat_copy = send([to(other, stat1, rstat1, ss1.at[0], rs1.at[0])])
    weights = wts[...]
    copies1 = {}

    def numerator(j):
        made = jnp.dot(weights, tok[:, j * cols:(j + 1) * cols], preferred_element_type=F32)
        made = made.astype(BF16).astype(F32).reshape(n_z, 2, per_dev, cols)
        for side in range(2):
            num1[j, side] = made[:, side].reshape(n_z * per_dev, cols).astype(BF16)
        copies1[j] = send([to(other, num1.at[j, 1 - c], rnum1.at[j], s1.at[j], r1.at[j])])

    def over_core(j):
        arrive(copies1[j])
        joint = mine * num1[j, c].astype(F32) + theirs * rnum1[j].astype(F32)
        send2[j] = fold(joint.reshape(n_z, per_dev, cols)).astype(BF16)
        send([
            to(z_ids[i], send2.at[j, z_to[i]], recv2.at[j, i], s2.at[j, i], r2.at[j])
            for i in z_far
        ])

    def over_z(j):
        arrive_all(recv2.at[j, pl.ds(1, n_z - 1)], r2.at[j])
        value = z_scales[0] * send2[j, z].astype(F32)
        for i in range(1, n_z):
            value = value + z_scales[i] * recv2[j, i].astype(F32)
        send3[j] = value.astype(BF16)
        send([
            to(dp_ids[i], send3.at[j], recv3.at[j, i], s3.at[j, i], r3.at[j]) for i in dp_far
        ])

    numerator(0)
    numerator(1)
    arrive(stat_copy)
    high, low, scales = join([stat1[...], rstat1[...]])
    stat2[...] = jnp.where(stat_row == 0, high, low)
    send([
        to(z_ids[i], stat2, rstat2.at[i], ss2.at[i], rs2) for i in z_far
    ])
    mine, theirs = [of_core(as_column(scale)) for scale in scales]
    over_core(0)
    for j in range(2, strips):
        numerator(j)
        over_core(j - 1)
    over_core(strips - 1)

    raw = logits[...]
    risen = jnp.exp(raw - jnp.max(raw, axis=0, keepdims=True))
    mix[...] = (risen / jnp.sum(risen, axis=0, keepdims=True)).T.astype(BF16)

    arrive_all(rstat2.at[pl.ds(1, n_z - 1)], rs2)
    high, low, scales = join([stat2[...]] + [rstat2[i] for i in range(1, n_z)])
    stat3[...] = jnp.where(stat_row == 0, high, low)
    send([
        to(dp_ids[i], stat3, rstat3.at[i], ss3.at[i], rs3) for i in dp_far
    ])
    z_scales = [own_column(scale) for scale in scales]
    for j in range(strips):
        over_z(j)
    arrive_all(rstat3.at[pl.ds(1, n_dp - 1)], rs3)
    high, low, scales = join([stat3[...]] + [rstat3[i] for i in range(1, n_dp)])
    dp_scales = [own_column(scale / low) for scale in scales]
    for load in load_in:
        load.wait()
    sums = [jnp.zeros((per_dev, hid), F32) for _ in range(exp_dev)]
    for j in range(strips):
        arrive_all(recv3.at[j, pl.ds(1, n_dp - 1)], r3.at[j])
        value = dp_scales[0] * send3[j].astype(F32)
        for i in range(1, n_dp):
            value = value + dp_scales[i] * recv3[j, i].astype(F32)
        x = unfold(value).astype(BF16)
        for e in range(exp_dev):
            sums[e] = sums[e] + jnp.dot(
                x, win[e, j * cols:(j + 1) * cols, :], preferred_element_type=F32
            )

    hidden = [gelu(total).astype(BF16) for total in sums]
    for load in load_out:
        load.wait()
    own_slots = per_dev // exp_dev
    owner = lax.broadcasted_iota(jnp.int32, (per_dev, cols), 0) // own_slots
    copies5 = {}
    early = list(sent)
    sent.clear()
    for j in range(strips):
        value = jnp.zeros((per_dev, cols), F32)
        for e in range(exp_dev):
            made = jnp.dot(
                hidden[e], wout[e, :, j * cols:(j + 1) * cols], preferred_element_type=F32
            )
            value = jnp.where(owner == e, made, value)
        part[j] = fold(value).astype(BF16)
        send([
            to(dp_ids[i], part.at[j], rpart.at[j, i], s4.at[j, i], r4.at[j]) for i in dp_far
        ])

    def to_core(src, j, i):
        send([to(other, src, recv6.at[j, i], s6.at[j, i], r6.at[j])])

    for copy in early:
        copy.wait_send()
    for j in range(strips):
        arrive_all(rpart.at[j, pl.ds(1, n_dp - 1)], r4.at[j])
        value = part[j].astype(F32)
        for i in range(1, n_dp):
            value = value + rpart[j, i].astype(F32)
        own5[j] = value.astype(BF16)
        copies5[j] = {
            i: send([to(z_ids[i], own5.at[j], recv5.at[j, i], s5.at[j, i], r5.at[j, i])])
            for i in z_far
        }
        to_core(own5.at[j], j, 0)
    mixing = mix[...]
    late = sent[:(n_dp - 1) * strips]
    del sent[:(n_dp - 1) * strips]
    for copy in late:
        copy.wait_send()

    def pass_on(j):
        for i in range(1, n_z):
            arrive(copies5[j][i])
            to_core(recv5.at[j, i], j, i)

    def mixed(j):
        arrive_all(recv6.at[j], r6.at[j])
        for i in range(n_z):
            tab[z_from[i], c] = recv5[j, i] if i else own5[j]
            tab[z_from[i], 1 - c] = recv6[j, i]
        table = unfold(tab[...].astype(F32).reshape(n_ex, 2 * per_dev, cols // 2))
        table = table.reshape(slots, cols).astype(BF16)
        out_ref[:, j * cols:(j + 1) * cols] = jnp.dot(
            mixing, table, preferred_element_type=F32
        ).astype(BF16)

    pass_on(0)
    for j in range(1, strips):
        pass_on(j)
        mixed(j - 1)
    drain()
    mixed(strips - 1)


def local(n_dp, n_ex, tokens, slot_param, pattern, w_in, w_out):
    rows, width = tokens.shape
    slots = slot_param.shape[1]
    per_dev = slots // n_ex
    lanes = -(-slots // 128) * 128
    n_z = n_ex // 2
    pieces, strips = 4, 4
    cols = width // strips
    flat = (2 * per_dev, cols // 2)
    dma = pltpu.SemaphoreType.DMA
    in_hbm = pl.BlockSpec(memory_space=pltpu.HBM)
    operands = (tokens, slot_param.T, pattern.T, w_in, w_out)
    placed = [pltpu.with_memory_space_constraint(x, pltpu.HBM) for x in operands]
    scratch = [
        ((slots, width), BF16),
        ((width, slots), BF16),
        ((slots, rows), F32),
        (pattern.shape[::-1], pattern.dtype),
        ((rows, width), BF16),
        (w_in.shape, BF16),
        (w_out.shape, BF16),
        ((slots, rows), F32),
        ((slots, rows), BF16),
        ((rows, slots), BF16),
        ((8, lanes), F32),
        ((8, lanes), F32),
        ((8, lanes), F32),
        ((n_z, 8, lanes), F32),
        ((8, lanes), F32),
        ((n_dp, 8, lanes), F32),
        ((strips, 2, n_z * per_dev, cols), BF16),
        ((strips, n_z * per_dev, cols), BF16),
        ((strips, n_z) + flat, BF16),
        ((strips, n_z) + flat, BF16),
        ((strips,) + flat, BF16),
        ((strips, n_dp) + flat, BF16),
        ((strips,) + flat, BF16),
        ((strips, n_dp) + flat, BF16),
        ((strips,) + flat, BF16),
        ((strips, n_z) + flat, BF16),
        ((strips, n_z) + flat, BF16),
        ((n_z, 2) + flat, BF16),
    ]
    by_z, by_dp = (strips, n_z), (strips, n_dp)
    leave = [(1,), (n_z,), (n_dp,), (strips,), by_z, by_dp, by_dp, by_z, by_z]
    come = [(1,), None, None, (strips,), (strips,), (strips,), (strips,), by_z, (strips,)]
    return pl.pallas_call(
        functools.partial(slots_kernel, n_dp, n_ex, pieces, strips),
        out_shape=jax.ShapeDtypeStruct((rows, width), BF16),
        in_specs=[in_hbm] * 5,
        out_specs=pl.BlockSpec(memory_space=pltpu.VMEM),
        scratch_shapes=[pltpu.VMEM(*one) for one in scratch]
        + [dma((pieces,)), dma((4 * w_in.shape[0],)), dma((2,))]
        + [dma(shape) if shape else dma for pair in zip(leave, come) for shape in pair],
        compiler_params=pltpu.CompilerParams(
            collective_id=0, has_side_effects=True, vmem_limit_bytes=48 * 1024 * 1024
        ),
        cost_estimate=pl.CostEstimate(
            flops=6 * rows * width * slots + 4 * per_dev * w_in.size // w_in.shape[0],
            bytes_accessed=2 * (tokens.size + w_in.size + w_out.size),
            transcendentals=2 * rows * slots,
        ),
    )(*placed)


def solution(mesh):
    return jax.shard_map(
        functools.partial(local, mesh.shape["dp"], mesh.shape["expert"]),
        mesh=mesh,
        in_specs=(
            P(("dp", "expert"), None),
            P(),
            P(None, ("dp", "expert")),
            P("expert", None, "dp"),
            P("expert", "dp", None),
        ),
        out_specs=P(("dp", "expert"), None),
        check_vma=False,
    )
```

```python
import functools

import jax
import jax.numpy as jnp
from jax import lax
from jax.experimental import pallas as pl
from jax.experimental.pallas import tpu as pltpu
from jax.sharding import PartitionSpec as P

MESH = pl.DeviceIdType.MESH
floor_value = -1e30
F32, BF16 = jnp.float32, jnp.bfloat16


def gelu(x):
    return 0.5 * x * (1.0 + jnp.tanh(0.7978845608028654 * (x + 0.044715 * (x * x * x))))


def fold(x):
    half = x.shape[-1] // 2
    return jnp.concatenate([x[..., :half], x[..., half:]], axis=x.ndim - 2)


def unfold(x):
    rows = x.shape[-2] // 2
    return jnp.concatenate([x[..., :rows, :], x[..., rows:, :]], axis=x.ndim - 1)


def flip(me, i, n):
    if n & (n - 1):
        return lax.rem(me + i, n), lax.rem(me + n - i, n)
    other, bit = 0, 1
    while bit < n:
        own = lax.rem(me // bit, 2)
        other = other + bit * ((1 - own) if i & bit else own)
        bit *= 2
    return other, other


def slots_kernel(
    n_dp, n_ex, pieces, strips,
    tok_hbm, slot_hbm, pat_hbm, win_hbm, wout_hbm,
    out_ref,
    slot_ref, slot_in, mask, pat_ref, tok, win, wout, logits, wts, mix, stat1, rstat1, stat2, rstat2, stat3, rstat3,
    num1, rnum1, send2, recv2, send3, recv3, part, rpart, own5, recv5, recv6, tab,
    tok_sem, w_sem, a_sem,
    ss1, rs1, ss2, rs2, ss3, rs3, s1, r1, s2, r2, s3, r3, s4, r4, s5, r5, s6, r6,
):
    d, k = lax.axis_index("dp"), lax.axis_index("expert")
    n_z = n_ex // 2
    z, c = k // 2, lax.rem(k, 2)
    slots, width = slot_ref.shape
    rows = tok.shape[0]
    cols = width // strips
    per_dev = slots // n_ex
    exp_dev, _, hid = win.shape
    blocks = pat_ref.shape[0]
    block = rows // blocks
    lanes = stat1.shape[1]
    piece = rows // pieces
    dp_to, _ = zip(*[flip(d, i, n_dp) for i in range(n_dp)])
    z_to, z_from = zip(*[flip(z, i, n_z) for i in range(n_z)])
    dp_far = list(range(n_dp - 1, 0, -1))
    z_far = list(range(n_z - 1, 0, -1))
    other = {"expert": 2 * z + 1 - c}
    dp_ids = [{"dp": target} for target in dp_to]
    z_ids = [{"expert": 2 * target + c} for target in z_to]

    def to(target, src, dst, ssem, rsem):
        return pltpu.make_async_remote_copy(
            src_ref=src, dst_ref=dst, send_sem=ssem, recv_sem=rsem,
            device_id=target, device_id_type=MESH,
        )

    sent = []

    def launch(copies):
        for copy in copies:
            copy.start()
        return copies

    def send(copies):
        sent.extend(copies)
        return launch(copies)

    def arrive(copies):
        for copy in copies:
            copy.wait_recv()

    def arrive_all(landed, sem):
        pltpu.make_async_copy(landed, landed, sem).wait()

    def drain():
        while sent:
            sent.pop(0).wait_send()

    loads = [
        pltpu.make_async_copy(
            tok_hbm.at[pl.ds(p * piece, piece)], tok.at[pl.ds(p * piece, piece)], tok_sem.at[p]
        )
        for p in range(pieces)
    ]
    load_slot = pltpu.make_async_copy(slot_hbm, slot_ref, a_sem.at[0])
    load_pat = pltpu.make_async_copy(pat_hbm, pat_ref, a_sem.at[1])
    launch([load_slot, load_pat] + loads)
    barrier = pltpu.get_barrier_semaphore()
    for target in [other] + dp_ids[1:] + z_ids[1:]:
        pl.semaphore_signal(barrier, inc=1, device_id=target, device_id_type=MESH)

    def in_parts(src, dst, first):
        depth = src.shape[1] // 2
        return [
            pltpu.make_async_copy(
                src.at[e, pl.ds(h * depth, depth)], dst.at[e, pl.ds(h * depth, depth)],
                w_sem.at[first + 2 * e + h],
            )
            for e in range(exp_dev) for h in range(2)
        ]

    load_in = in_parts(win_hbm, win, 0)
    load_out = in_parts(wout_hbm, wout, 2 * exp_dev)

    row_id = lax.broadcasted_iota(jnp.int32, (slots, lanes), 0)
    lane_id = lax.broadcasted_iota(jnp.int32, (slots, lanes), 1)
    eye = row_id == lane_id

    def as_column(row):
        return jnp.sum(jnp.where(eye, row, 0.0), axis=1, keepdims=True)

    own_shape = (2 * per_dev, lanes)
    own_row = lax.rem(lax.broadcasted_iota(jnp.int32, own_shape, 0), per_dev) + k * per_dev
    own_eye = own_row == lax.broadcasted_iota(jnp.int32, own_shape, 1)

    def own_column(row):
        return jnp.sum(jnp.where(own_eye, row, 0.0), axis=1, keepdims=True)

    def of_core(x):
        x = x.reshape(n_z, 2, per_dev, x.shape[-1])
        return jnp.where(c == 0, x[:, 0], x[:, 1]).reshape(n_z * per_dev, x.shape[-1])

    def as_row(column):
        return jnp.sum(jnp.where(eye, column, 0.0), axis=0, keepdims=True)

    load_slot.wait()
    load_pat.wait()
    slot_in[...] = slot_ref[...].astype(F32).T.astype(BF16)
    seen = pat_ref[...].astype(F32)
    if lanes > slots:
        seen = jnp.concatenate([seen, jnp.zeros((blocks, lanes - slots), F32)], axis=1)
    for b in range(blocks):
        mask[:, b * block:(b + 1) * block] = jnp.broadcast_to(
            as_column(seen[b:b + 1, :]), (slots, block)
        )

    top = jnp.full((slots, piece), floor_value, F32)
    for p in range(pieces):
        loads[p].wait()
        if p == pieces - 1:
            launch(load_in + load_out)
        span = slice(p * piece, (p + 1) * piece)
        made = jnp.dot(tok[span, :], slot_in[...], preferred_element_type=F32).T
        logits[:, span] = made
        top = jnp.maximum(top, jnp.where(mask[:, span] > 0.0, made, floor_value))
    peak = jnp.max(top, axis=1, keepdims=True)
    raw = logits[...]
    shifted = jnp.where(mask[...] > 0.0, raw - peak, floor_value)
    weights = jnp.exp(shifted).astype(BF16)
    wts[...] = weights
    den = jnp.sum(weights.astype(F32), axis=1, keepdims=True)
    stat_row = lax.broadcasted_iota(jnp.int32, stat1.shape, 0)
    stat1[...] = jnp.where(stat_row == 0, as_row(peak), as_row(den))

    def join(stats):
        high = stats[0][0:1]
        for stat in stats[1:]:
            high = jnp.maximum(high, stat[0:1])
        scales = [jnp.exp(stat[0:1] - high) for stat in stats]
        low = stats[0][1:2] * scales[0]
        for stat, scale in zip(stats[1:], scales[1:]):
            low = low + stat[1:2] * scale
        return high, low, scales

    pl.semaphore_wait(barrier, n_dp - 1 + n_z)
    stat_copy = send([to(other, stat1, rstat1, ss1.at[0], rs1.at[0])])
    weights = wts[...]
    copies1 = {}

    def numerator(j):
        made = jnp.dot(weights, tok[:, j * cols:(j + 1) * cols], preferred_element_type=F32)
        made = made.astype(BF16).astype(F32).reshape(n_z, 2, per_dev, cols)
        for side in range(2):
            num1[j, side] = made[:, side].reshape(n_z * per_dev, cols).astype(BF16)
        copies1[j] = send([to(other, num1.at[j, 1 - c], rnum1.at[j], s1.at[j], r1.at[j])])

    def over_core(j):
        arrive(copies1[j])
        joint = mine * num1[j, c].astype(F32) + theirs * rnum1[j].astype(F32)
        send2[j] = fold(joint.reshape(n_z, per_dev, cols)).astype(BF16)
        send([
            to(z_ids[i], send2.at[j, z_to[i]], recv2.at[j, i], s2.at[j, i], r2.at[j])
            for i in z_far
        ])

    def over_z(j):
        arrive_all(recv2.at[j, pl.ds(1, n_z - 1)], r2.at[j])
        value = z_scales[0] * send2[j, z].astype(F32)
        for i in range(1, n_z):
            value = value + z_scales[i] * recv2[j, i].astype(F32)
        send3[j] = value.astype(BF16)
        send([
            to(dp_ids[i], send3.at[j], recv3.at[j, i], s3.at[j, i], r3.at[j]) for i in dp_far
        ])

    numerator(0)
    numerator(1)
    arrive(stat_copy)
    high, low, scales = join([stat1[...], rstat1[...]])
    stat2[...] = jnp.where(stat_row == 0, high, low)
    send([
        to(z_ids[i], stat2, rstat2.at[i], ss2.at[i], rs2) for i in z_far
    ])
    mine, theirs = [of_core(as_column(scale)) for scale in scales]
    over_core(0)
    for j in range(2, strips):
        numerator(j)
        over_core(j - 1)
    over_core(strips - 1)

    raw = logits[...]
    risen = jnp.exp(raw - jnp.max(raw, axis=0, keepdims=True))
    mix[...] = (risen / jnp.sum(risen, axis=0, keepdims=True)).T.astype(BF16)

    arrive_all(rstat2.at[pl.ds(1, n_z - 1)], rs2)
    high, low, scales = join([stat2[...]] + [rstat2[i] for i in range(1, n_z)])
    stat3[...] = jnp.where(stat_row == 0, high, low)
    send([
        to(dp_ids[i], stat3, rstat3.at[i], ss3.at[i], rs3) for i in dp_far
    ])
    z_scales = [own_column(scale) for scale in scales]
    for j in range(strips):
        over_z(j)
    arrive_all(rstat3.at[pl.ds(1, n_dp - 1)], rs3)
    high, low, scales = join([stat3[...]] + [rstat3[i] for i in range(1, n_dp)])
    dp_scales = [own_column(scale / low) for scale in scales]
    for load in load_in:
        load.wait()
    sums = [jnp.zeros((per_dev, hid), F32) for _ in range(exp_dev)]
    for j in range(strips):
        arrive_all(recv3.at[j, pl.ds(1, n_dp - 1)], r3.at[j])
        value = dp_scales[0] * send3[j].astype(F32)
        for i in range(1, n_dp):
            value = value + dp_scales[i] * recv3[j, i].astype(F32)
        x = unfold(value).astype(BF16)
        for e in range(exp_dev):
            sums[e] = sums[e] + jnp.dot(
                x, win[e, j * cols:(j + 1) * cols, :], preferred_element_type=F32
            )

    hidden = [gelu(total).astype(BF16) for total in sums]
    for load in load_out:
        load.wait()
    own_slots = per_dev // exp_dev
    owner = lax.broadcasted_iota(jnp.int32, (per_dev, cols), 0) // own_slots
    copies5 = {}
    early = list(sent)
    sent.clear()
    for j in range(strips):
        value = jnp.zeros((per_dev, cols), F32)
        for e in range(exp_dev):
            made = jnp.dot(
                hidden[e], wout[e, :, j * cols:(j + 1) * cols], preferred_element_type=F32
            )
            value = jnp.where(owner == e, made, value)
        part[j] = fold(value).astype(BF16)
        send([
            to(dp_ids[i], part.at[j], rpart.at[j, i], s4.at[j, i], r4.at[j]) for i in dp_far
        ])

    def to_core(src, j, i):
        send([to(other, src, recv6.at[j, i], s6.at[j, i], r6.at[j])])

    for copy in early:
        copy.wait_send()
    for j in range(strips):
        arrive_all(rpart.at[j, pl.ds(1, n_dp - 1)], r4.at[j])
        value = part[j].astype(F32)
        for i in range(1, n_dp):
            value = value + rpart[j, i].astype(F32)
        own5[j] = value.astype(BF16)
        copies5[j] = {
            i: send([to(z_ids[i], own5.at[j], recv5.at[j, i], s5.at[j, i], r5.at[j, i])])
            for i in z_far
        }
        to_core(own5.at[j], j, 0)
    mixing = mix[...]
    late = sent[:(n_dp - 1) * strips]
    del sent[:(n_dp - 1) * strips]
    for copy in late:
        copy.wait_send()

    def pass_on(j):
        for i in range(1, n_z):
            arrive(copies5[j][i])
            to_core(recv5.at[j, i], j, i)

    def mixed(j):
        arrive_all(recv6.at[j], r6.at[j])
        for i in range(n_z):
            tab[z_from[i], c] = recv5[j, i] if i else own5[j]
            tab[z_from[i], 1 - c] = recv6[j, i]
        table = unfold(tab[...].astype(F32).reshape(n_ex, 2 * per_dev, cols // 2))
        table = table.reshape(slots, cols).astype(BF16)
        out_ref[:, j * cols:(j + 1) * cols] = jnp.dot(
            mixing, table, preferred_element_type=F32
        ).astype(BF16)

    pass_on(0)
    for j in range(1, strips):
        pass_on(j)
        mixed(j - 1)
    drain()
    mixed(strips - 1)


def local(n_dp, n_ex, tokens, slot_param, pattern, w_in, w_out):
    rows, width = tokens.shape
    slots = slot_param.shape[1]
    per_dev = slots // n_ex
    lanes = -(-slots // 128) * 128
    n_z = n_ex // 2
    pieces, strips = 4, 8
    cols = width // strips
    flat = (2 * per_dev, cols // 2)
    dma = pltpu.SemaphoreType.DMA
    in_hbm = pl.BlockSpec(memory_space=pltpu.HBM)
    operands = (tokens, slot_param.T, pattern.T, w_in, w_out)
    placed = [pltpu.with_memory_space_constraint(x, pltpu.HBM) for x in operands]
    scratch = [
        ((slots, width), BF16),
        ((width, slots), BF16),
        ((slots, rows), F32),
        (pattern.shape[::-1], pattern.dtype),
        ((rows, width), BF16),
        (w_in.shape, BF16),
        (w_out.shape, BF16),
        ((slots, rows), F32),
        ((slots, rows), BF16),
        ((rows, slots), BF16),
        ((8, lanes), F32),
        ((8, lanes), F32),
        ((8, lanes), F32),
        ((n_z, 8, lanes), F32),
        ((8, lanes), F32),
        ((n_dp, 8, lanes), F32),
        ((strips, 2, n_z * per_dev, cols), BF16),
        ((strips, n_z * per_dev, cols), BF16),
        ((strips, n_z) + flat, BF16),
        ((strips, n_z) + flat, BF16),
        ((strips,) + flat, BF16),
        ((strips, n_dp) + flat, BF16),
        ((strips,) + flat, BF16),
        ((strips, n_dp) + flat, BF16),
        ((strips,) + flat, BF16),
        ((strips, n_z) + flat, BF16),
        ((strips, n_z) + flat, BF16),
        ((n_z, 2) + flat, BF16),
    ]
    by_z, by_dp = (strips, n_z), (strips, n_dp)
    leave = [(1,), (n_z,), (n_dp,), (strips,), by_z, by_dp, by_dp, by_z, by_z]
    come = [(1,), None, None, (strips,), (strips,), (strips,), (strips,), by_z, (strips,)]
    return pl.pallas_call(
        functools.partial(slots_kernel, n_dp, n_ex, pieces, strips),
        out_shape=jax.ShapeDtypeStruct((rows, width), BF16),
        in_specs=[in_hbm] * 5,
        out_specs=pl.BlockSpec(memory_space=pltpu.VMEM),
        scratch_shapes=[pltpu.VMEM(*one) for one in scratch]
        + [dma((pieces,)), dma((4 * w_in.shape[0],)), dma((2,))]
        + [dma(shape) if shape else dma for pair in zip(leave, come) for shape in pair],
        compiler_params=pltpu.CompilerParams(
            collective_id=0, has_side_effects=True, vmem_limit_bytes=48 * 1024 * 1024
        ),
        cost_estimate=pl.CostEstimate(
            flops=6 * rows * width * slots + 4 * per_dev * w_in.size // w_in.shape[0],
            bytes_accessed=2 * (tokens.size + w_in.size + w_out.size),
            transcendentals=2 * rows * slots,
        ),
    )(*placed)


def solution(mesh):
    return jax.shard_map(
        functools.partial(local, mesh.shape["dp"], mesh.shape["expert"]),
        mesh=mesh,
        in_specs=(
            P(("dp", "expert"), None),
            P(),
            P(None, ("dp", "expert")),
            P("expert", None, "dp"),
            P("expert", "dp", None),
        ),
        out_specs=P(("dp", "expert"), None),
        check_vma=False,
    )
```

```python
import functools

import jax
import jax.numpy as jnp
from jax import lax
from jax.experimental import pallas as pl
from jax.experimental.pallas import tpu as pltpu
from jax.sharding import PartitionSpec as P

MESH = pl.DeviceIdType.MESH
floor_value = -1e30
F32, BF16 = jnp.float32, jnp.bfloat16


def gelu(x):
    return 0.5 * x * (1.0 + jnp.tanh(0.7978845608028654 * (x + 0.044715 * (x * x * x))))


def fold(x):
    half = x.shape[-1] // 2
    return jnp.concatenate([x[..., :half], x[..., half:]], axis=x.ndim - 2)


def unfold(x):
    rows = x.shape[-2] // 2
    return jnp.concatenate([x[..., :rows, :], x[..., rows:, :]], axis=x.ndim - 1)


def flip(me, i, n):
    if n & (n - 1):
        return lax.rem(me + i, n), lax.rem(me + n - i, n)
    other, bit = 0, 1
    while bit < n:
        own = lax.rem(me // bit, 2)
        other = other + bit * ((1 - own) if i & bit else own)
        bit *= 2
    return other, other


def slots_kernel(
    n_dp, n_ex, pieces, strips,
    tok_hbm, slot_hbm, pat_hbm, win_hbm, wout_hbm,
    out_ref,
    slot_ref, slot_in, mask, pat_ref, tok, win, wout, logits, wts, mix, stat1, rstat1, stat2, rstat2, stat3, rstat3,
    num1, rnum1, send2, recv2, send3, recv3, part, rpart, recv5, recv6, tab,
    tok_sem, w_sem, a_sem,
    ss1, rs1, ss2, rs2, ss3, rs3, s1, r1, s2, r2, s3, r3, s4, r4, s5, r5, s6, r6,
):
    d, k = lax.axis_index("dp"), lax.axis_index("expert")
    n_z = n_ex // 2
    z, c = k // 2, lax.rem(k, 2)
    slots, width = slot_ref.shape
    rows = tok.shape[0]
    cols = width // strips
    per_dev = slots // n_ex
    exp_dev, _, hid = win.shape
    blocks = pat_ref.shape[0]
    block = rows // blocks
    lanes = stat1.shape[1]
    piece = rows // pieces
    dp_to, _ = zip(*[flip(d, i, n_dp) for i in range(n_dp)])
    z_to, z_from = zip(*[flip(z, i, n_z) for i in range(n_z)])
    dp_far = list(range(n_dp - 1, 0, -1))
    z_far = list(range(n_z - 1, 0, -1))
    other = {"expert": 2 * z + 1 - c}
    dp_ids = [{"dp": target} for target in dp_to]
    z_ids = [{"expert": 2 * target + c} for target in z_to]

    def to(target, src, dst, ssem, rsem):
        return pltpu.make_async_remote_copy(
            src_ref=src, dst_ref=dst, send_sem=ssem, recv_sem=rsem,
            device_id=target, device_id_type=MESH,
        )

    sent = []

    def launch(copies):
        for copy in copies:
            copy.start()
        return copies

    def send(copies):
        sent.extend(copies)
        return launch(copies)

    def arrive(copies):
        for copy in copies:
            copy.wait_recv()

    def arrive_all(landed, sem):
        pltpu.make_async_copy(landed, landed, sem).wait()

    def drain():
        while sent:
            sent.pop(0).wait_send()

    loads = [
        pltpu.make_async_copy(
            tok_hbm.at[pl.ds(p * piece, piece)], tok.at[pl.ds(p * piece, piece)], tok_sem.at[p]
        )
        for p in range(pieces)
    ]
    load_slot = pltpu.make_async_copy(slot_hbm, slot_ref, a_sem.at[0])
    load_pat = pltpu.make_async_copy(pat_hbm, pat_ref, a_sem.at[1])
    launch([load_slot, load_pat] + loads)
    barrier = pltpu.get_barrier_semaphore()
    for target in [other] + dp_ids[1:] + z_ids[1:]:
        pl.semaphore_signal(barrier, inc=1, device_id=target, device_id_type=MESH)

    def in_parts(src, dst, first):
        depth = src.shape[1] // 2
        return [
            pltpu.make_async_copy(
                src.at[e, pl.ds(h * depth, depth)], dst.at[e, pl.ds(h * depth, depth)],
                w_sem.at[first + 2 * e + h],
            )
            for e in range(exp_dev) for h in range(2)
        ]

    load_in = in_parts(win_hbm, win, 0)
    load_out = in_parts(wout_hbm, wout, 2 * exp_dev)

    row_id = lax.broadcasted_iota(jnp.int32, (slots, lanes), 0)
    lane_id = lax.broadcasted_iota(jnp.int32, (slots, lanes), 1)
    eye = row_id == lane_id

    def as_column(row):
        return jnp.sum(jnp.where(eye, row, 0.0), axis=1, keepdims=True)

    own_shape = (2 * per_dev, lanes)
    own_row = lax.rem(lax.broadcasted_iota(jnp.int32, own_shape, 0), per_dev) + k * per_dev
    own_eye = own_row == lax.broadcasted_iota(jnp.int32, own_shape, 1)

    def own_column(row):
        return jnp.sum(jnp.where(own_eye, row, 0.0), axis=1, keepdims=True)

    def of_core(x):
        x = x.reshape(n_z, 2, per_dev, x.shape[-1])
        return jnp.where(c == 0, x[:, 0], x[:, 1]).reshape(n_z * per_dev, x.shape[-1])

    def as_row(column):
        return jnp.sum(jnp.where(eye, column, 0.0), axis=0, keepdims=True)

    load_slot.wait()
    load_pat.wait()
    slot_in[...] = slot_ref[...].astype(F32).T.astype(BF16)
    seen = pat_ref[...].astype(F32)
    if lanes > slots:
        seen = jnp.concatenate([seen, jnp.zeros((blocks, lanes - slots), F32)], axis=1)
    for b in range(blocks):
        mask[:, b * block:(b + 1) * block] = jnp.broadcast_to(
            as_column(seen[b:b + 1, :]), (slots, block)
        )

    top = jnp.full((slots, piece), floor_value, F32)
    for p in range(pieces):
        loads[p].wait()
        if p == pieces - 1:
            launch(load_in + load_out)
        span = slice(p * piece, (p + 1) * piece)
        made = jnp.dot(tok[span, :], slot_in[...], preferred_element_type=F32).T
        logits[:, span] = made
        top = jnp.maximum(top, jnp.where(mask[:, span] > 0.0, made, floor_value))
    peak = jnp.max(top, axis=1, keepdims=True)
    raw = logits[...]
    shifted = jnp.where(mask[...] > 0.0, raw - peak, floor_value)
    weights = jnp.exp(shifted).astype(BF16)
    wts[...] = weights
    den = jnp.sum(weights.astype(F32), axis=1, keepdims=True)
    stat_row = lax.broadcasted_iota(jnp.int32, stat1.shape, 0)
    stat1[...] = jnp.where(stat_row == 0, as_row(peak), as_row(den))

    def join(stats):
        high = stats[0][0:1]
        for stat in stats[1:]:
            high = jnp.maximum(high, stat[0:1])
        scales = [jnp.exp(stat[0:1] - high) for stat in stats]
        low = stats[0][1:2] * scales[0]
        for stat, scale in zip(stats[1:], scales[1:]):
            low = low + stat[1:2] * scale
        return high, low, scales

    pl.semaphore_wait(barrier, n_dp - 1 + n_z)
    stat_copy = send([to(other, stat1, rstat1, ss1.at[0], rs1.at[0])])
    weights = wts[...]
    copies1 = {}

    def numerator(j):
        made = jnp.dot(weights, tok[:, j * cols:(j + 1) * cols], preferred_element_type=F32)
        made = made.astype(BF16).astype(F32).reshape(n_z, 2, per_dev, cols)
        for side in range(2):
            num1[j, side] = made[:, side].reshape(n_z * per_dev, cols).astype(BF16)
        copies1[j] = send([to(other, num1.at[j, 1 - c], rnum1.at[j], s1.at[j], r1.at[j])])

    def over_core(j):
        arrive(copies1[j])
        joint = mine * num1[j, c].astype(F32) + theirs * rnum1[j].astype(F32)
        send2[j] = fold(joint.reshape(n_z, per_dev, cols)).astype(BF16)
        send([
            to(z_ids[i], send2.at[j, z_to[i]], recv2.at[j, i], s2.at[j, i], r2.at[j])
            for i in z_far
        ])

    def over_z(j):
        arrive_all(recv2.at[j, pl.ds(1, n_z - 1)], r2.at[j])
        value = z_scales[0] * send2[j, z].astype(F32)
        for i in range(1, n_z):
            value = value + z_scales[i] * recv2[j, i].astype(F32)
        send3[j] = value.astype(BF16)
        send([
            to(dp_ids[i], send3.at[j], recv3.at[j, i], s3.at[j, i], r3.at[j]) for i in dp_far
        ])

    numerator(0)
    numerator(1)
    arrive(stat_copy)
    high, low, scales = join([stat1[...], rstat1[...]])
    stat2[...] = jnp.where(stat_row == 0, high, low)
    send([
        to(z_ids[i], stat2, rstat2.at[i], ss2.at[i], rs2) for i in z_far
    ])
    mine, theirs = [of_core(as_column(scale)) for scale in scales]
    over_core(0)
    for j in range(2, strips):
        numerator(j)
        over_core(j - 1)
    over_core(strips - 1)

    raw = logits[...]
    risen = jnp.exp(raw - jnp.max(raw, axis=0, keepdims=True))
    mix[...] = (risen / jnp.sum(risen, axis=0, keepdims=True)).T.astype(BF16)

    arrive_all(rstat2.at[pl.ds(1, n_z - 1)], rs2)
    high, low, scales = join([stat2[...]] + [rstat2[i] for i in range(1, n_z)])
    stat3[...] = jnp.where(stat_row == 0, high, low)
    send([
        to(dp_ids[i], stat3, rstat3.at[i], ss3.at[i], rs3) for i in dp_far
    ])
    z_scales = [own_column(scale) for scale in scales]
    for j in range(strips):
        over_z(j)
    arrive_all(rstat3.at[pl.ds(1, n_dp - 1)], rs3)
    high, low, scales = join([stat3[...]] + [rstat3[i] for i in range(1, n_dp)])
    dp_scales = [own_column(scale / low) for scale in scales]
    for load in load_in:
        load.wait()
    sums = [jnp.zeros((per_dev, hid), F32) for _ in range(exp_dev)]
    for j in range(strips):
        arrive_all(recv3.at[j, pl.ds(1, n_dp - 1)], r3.at[j])
        value = dp_scales[0] * send3[j].astype(F32)
        for i in range(1, n_dp):
            value = value + dp_scales[i] * recv3[j, i].astype(F32)
        x = unfold(value).astype(BF16)
        for e in range(exp_dev):
            sums[e] = sums[e] + jnp.dot(
                x, win[e, j * cols:(j + 1) * cols, :], preferred_element_type=F32
            )

    hidden = [gelu(total).astype(BF16) for total in sums]
    for load in load_out:
        load.wait()
    own_slots = per_dev // exp_dev
    owner = lax.broadcasted_iota(jnp.int32, (per_dev, cols), 0) // own_slots
    copies5 = {}
    early = list(sent)
    sent.clear()
    for j in range(strips):
        value = jnp.zeros((per_dev, cols), F32)
        for e in range(exp_dev):
            made = jnp.dot(
                hidden[e], wout[e, :, j * cols:(j + 1) * cols], preferred_element_type=F32
            )
            value = jnp.where(owner == e, made, value)
        part[j] = fold(value).astype(BF16)
        send([
            to(dp_ids[i], part.at[j], rpart.at[j, i], s4.at[j, i], r4.at[j]) for i in dp_far
        ])

    for copy in early:
        copy.wait_send()
    for j in range(strips):
        arrive_all(rpart.at[j, pl.ds(1, n_dp - 1)], r4.at[j])
        value = part[j].astype(F32)
        for i in range(1, n_dp):
            value = value + rpart[j, i].astype(F32)
        recv5[j, 0] = value.astype(BF16)
        copies5[j] = {
            i: send([to(z_ids[i], recv5.at[j, 0], recv5.at[j, i], s5.at[j, i], r5.at[j, i])])
            for i in z_far
        }
    mixing = mix[...]
    late = sent[:(n_dp - 1) * strips]
    del sent[:(n_dp - 1) * strips]
    for copy in late:
        copy.wait_send()

    def pass_on(j):
        for i in range(1, n_z):
            arrive(copies5[j][i])
        send([to(other, recv5.at[j], recv6.at[j], s6.at[j], r6.at[j])])

    def mixed(j):
        arrive_all(recv6.at[j], r6.at[j])
        for i in range(n_z):
            tab[z_from[i], c] = recv5[j, i]
            tab[z_from[i], 1 - c] = recv6[j, i]
        table = unfold(tab[...].astype(F32).reshape(n_ex, 2 * per_dev, cols // 2))
        table = table.reshape(slots, cols).astype(BF16)
        out_ref[:, j * cols:(j + 1) * cols] = jnp.dot(
            mixing, table, preferred_element_type=F32
        ).astype(BF16)

    pass_on(0)
    for j in range(1, strips):
        pass_on(j)
        mixed(j - 1)
    drain()
    mixed(strips - 1)


def local(n_dp, n_ex, tokens, slot_param, pattern, w_in, w_out):
    rows, width = tokens.shape
    slots = slot_param.shape[1]
    per_dev = slots // n_ex
    lanes = -(-slots // 128) * 128
    n_z = n_ex // 2
    pieces, strips = 4, 4
    cols = width // strips
    flat = (2 * per_dev, cols // 2)
    dma = pltpu.SemaphoreType.DMA
    in_hbm = pl.BlockSpec(memory_space=pltpu.HBM)
    operands = (tokens, slot_param.T, pattern.T, w_in, w_out)
    placed = [pltpu.with_memory_space_constraint(x, pltpu.HBM) for x in operands]
    scratch = [
        ((slots, width), BF16),
        ((width, slots), BF16),
        ((slots, rows), F32),
        (pattern.shape[::-1], pattern.dtype),
        ((rows, width), BF16),
        (w_in.shape, BF16),
        (w_out.shape, BF16),
        ((slots, rows), F32),
        ((slots, rows), BF16),
        ((rows, slots), BF16),
        ((8, lanes), F32),
        ((8, lanes), F32),
        ((8, lanes), F32),
        ((n_z, 8, lanes), F32),
        ((8, lanes), F32),
        ((n_dp, 8, lanes), F32),
        ((strips, 2, n_z * per_dev, cols), BF16),
        ((strips, n_z * per_dev, cols), BF16),
        ((strips, n_z) + flat, BF16),
        ((strips, n_z) + flat, BF16),
        ((strips,) + flat, BF16),
        ((strips, n_dp) + flat, BF16),
        ((strips,) + flat, BF16),
        ((strips, n_dp) + flat, BF16),
        ((strips, n_z) + flat, BF16),
        ((strips, n_z) + flat, BF16),
        ((n_z, 2) + flat, BF16),
    ]
    by_z, by_dp = (strips, n_z), (strips, n_dp)
    leave = [(1,), (n_z,), (n_dp,), (strips,), by_z, by_dp, by_dp, by_z, (strips,)]
    come = [(1,), None, None, (strips,), (strips,), (strips,), (strips,), by_z, (strips,)]
    return pl.pallas_call(
        functools.partial(slots_kernel, n_dp, n_ex, pieces, strips),
        out_shape=jax.ShapeDtypeStruct((rows, width), BF16),
        in_specs=[in_hbm] * 5,
        out_specs=pl.BlockSpec(memory_space=pltpu.VMEM),
        scratch_shapes=[pltpu.VMEM(*one) for one in scratch]
        + [dma((pieces,)), dma((4 * w_in.shape[0],)), dma((2,))]
        + [dma(shape) if shape else dma for pair in zip(leave, come) for shape in pair],
        compiler_params=pltpu.CompilerParams(
            collective_id=0, has_side_effects=True, vmem_limit_bytes=48 * 1024 * 1024
        ),
        cost_estimate=pl.CostEstimate(
            flops=6 * rows * width * slots + 4 * per_dev * w_in.size // w_in.shape[0],
            bytes_accessed=2 * (tokens.size + w_in.size + w_out.size),
            transcendentals=2 * rows * slots,
        ),
    )(*placed)


def solution(mesh):
    return jax.shard_map(
        functools.partial(local, mesh.shape["dp"], mesh.shape["expert"]),
        mesh=mesh,
        in_specs=(
            P(("dp", "expert"), None),
            P(),
            P(None, ("dp", "expert")),
            P("expert", None, "dp"),
            P("expert", "dp", None),
        ),
        out_specs=P(("dp", "expert"), None),
        check_vma=False,
    )
```
